32 devices in a mesh: ex: 8 (over y, x, core), feat: 4 (over z).
Axes of the slice: x: 2, y: 2, z: 4, core: 2. Of those that a mesh axis runs over, the one named last changes fastest.
Arguments:
- features: bfloat16 [16384, 2048], P('ex', 'feat'), may hold values from -0.125 to 0.125
- weights: float32 [2048], P('feat'), may hold values from -6 to 6
- labels: int32 [16384], P('ex'), may hold values 0 or 1
- signs: int32 [16384], P('ex'), may hold values from -1 to 1, as said below
- samples: int32 [2048], replicated, may hold values from 0 to 16383
- radius: float32 [1], replicated, may hold values from 0.1 to 0.25
Outputs:
- new_weights: float32 [2048], P('feat')
The draws below stay inside these ranges and needn't reach their ends.
Inputs may be any that keep to these rules, and one draw needn't show every extreme that they name: `signs`: each entry is -1 or +1.
All inputs are finite; a program needn't handle non-finite values. No bound on the sum of `labels` on one device may be relied on, other than what follows from the above.
Results may differ from the reference program's by a relative error of at most 0.00067.
Values may be sent and summed in bfloat16 or wider, within the bound.
No kernel may reach another device: no remote copies, remote signals or barrier semaphores. Data moves between devices by JAX's collectives and lax.ppermute only.
A program may use at most 192 MiB of HBM per device.

```python
import math
import jax
import jax.numpy as jnp
from jax import lax

D = 2048
M = 2048
ITERS = 4
N = 16384


def draw_signs(key, part):
    return (2 * jax.random.randint(key, (N,), 0, 2) - 1).astype(jnp.int32)


def touch_ends(array, own_key, smallest, top_value):
    extent = array.shape
    index_at = [jax.random.randint(jax.random.fold_in(own_key, axis), (), 0, extent[axis]) for axis in range(len(extent))]
    array = array.at[tuple(index_at)].set(smallest)
    longest = extent.index(max(extent))
    index_at[longest] = (index_at[longest] + 1) % extent[longest]
    return array.at[tuple(index_at)].set(top_value)


def levels(own_key, dims, shards, least, high):
    loudness = 1.0
    for axis_at, shards_of in shards:
        heights = jax.random.uniform(jax.random.fold_in(jax.random.fold_in(own_key, 6), axis_at), (shards_of,), jnp.float32, least / len(shards), high / len(shards))
        loudness = loudness * jnp.repeat(jnp.exp(heights), dims[axis_at] // shards_of).reshape((-1,) + (1,) * (len(dims) - 1 - axis_at))
    return loudness


def gaussian(rng, extent, width, most, pieces=(), held_as=jnp.bfloat16):
    level = levels(rng, extent, pieces, -0.22, 0.18) if pieces else 1.0
    array = jax.random.normal(rng, extent, jnp.float32) * width * level
    return jnp.minimum(jnp.maximum(array, -most), most).astype(held_as)


def setup_inputs(seed: int = 0) -> dict:
    seeds = jax.random.split(jax.random.key(seed), 7)
    return {
        "features": gaussian(seeds[0], (N, D), D ** -0.5, 0.125, ((0, 8), (1, 4))),
        "weights": gaussian(seeds[1], (D,), 1.0, 6.0, ((0, 4),), jnp.float32),
        "labels": touch_ends((jax.random.randint(seeds[2], (N,), 0, 2) < 1).astype(jnp.int32), jax.random.fold_in(seeds[2], 1), 0, 1),
        "signs": draw_signs(jax.random.fold_in(seeds[6], 71), 0),
        "samples": touch_ends(jax.random.randint(seeds[4], (M,), 0, N), jax.random.fold_in(seeds[4], 1), 0, N - 1).astype(jnp.int32),
        "radius": jnp.clip(jax.random.uniform(seeds[5], (1,), jnp.float32, 0.1, 0.25), 0.1, 0.25),
    }


REG = 0.02

def hadamard_rows(matrix):
    length = matrix.shape[0]
    stride = 1
    while stride < length:
        shaped = matrix.reshape(length // (2 * stride), 2, stride, matrix.shape[1])
        matrix = jnp.stack([shaped[:, 0] + shaped[:, 1], shaped[:, 0] - shaped[:, 1]], axis=1).reshape(length, matrix.shape[1])
        stride = stride * 2
    return matrix

def precondition(factor_lower, residual):
    middle = lax.linalg.triangular_solve(factor_lower, residual[:, None], left_side=True, lower=True)
    return lax.linalg.triangular_solve(factor_lower, middle, left_side=True, lower=True, transpose_a=True)[:, 0]

def reference(features, weights, labels, signs, samples, radius):
    highest = lax.Precision.HIGHEST
    dense = features.astype(jnp.float32)
    margins = jnp.dot(dense, weights, precision=highest)
    probability = 1.0 / (1.0 + jnp.exp(-margins))
    curvature = probability * (1.0 - probability)
    ridge = REG / D
    gradient = jnp.dot(probability - labels.astype(jnp.float32), dense, precision=highest) / N + ridge * weights
    weighted = (jnp.sqrt(curvature)[:, None] * dense).astype(jnp.bfloat16)
    weighted_float = weighted.astype(jnp.float32)
    mixed = hadamard_rows(weighted_float * signs.astype(jnp.float32)[:, None])
    sketch = (mixed[samples] * (1.0 / math.sqrt(N * M))).astype(jnp.bfloat16)
    gram = jnp.dot(sketch.T.astype(jnp.float32), sketch.astype(jnp.float32), preferred_element_type=jnp.float32) + ridge * jnp.eye(D, dtype=jnp.float32)
    factor_lower = jnp.linalg.cholesky(gram)
    solution = jnp.zeros((D,), jnp.float32)
    residual = -gradient
    solved = precondition(factor_lower, residual)
    inner_now = jnp.dot(residual, solved)
    direction = solved
    for number in range(ITERS):
        row_sums = jnp.dot(weighted_float, direction, precision=highest)
        curved = jnp.dot(row_sums, weighted_float, precision=highest) / N + ridge * direction
        step_size = inner_now / jnp.dot(direction, curved)
        solution = solution + step_size * direction
        residual = residual - step_size * curved
        solved = precondition(factor_lower, residual)
        inner_next = jnp.dot(residual, solved)
        direction = solved + inner_next / inner_now * direction
        inner_now = inner_next
    length_sq = jnp.dot(solution, solution)
    scale_step = jnp.minimum(1.0, radius[0] * math.sqrt(D) / jnp.sqrt(length_sq + 1e-06))
    return weights + scale_step * solution
```

```python
import math

import jax
import jax.numpy as jnp
from jax import lax
from jax.experimental import pallas as pl
from jax.experimental.pallas import tpu as pltpu
from jax.sharding import PartitionSpec as P

D = 2048
ITERS = 4
REG = 0.02
BLOCK = 128
PIVOTS = 8
CHUNK = 256


def split(value):
    high = value.astype(jnp.bfloat16)
    low = (value - high.astype(jnp.float32)).astype(jnp.bfloat16)
    return high, low


def invert_block(block):
    tiles = BLOCK // PIVOTS
    lane = lax.broadcasted_iota(jnp.int32, (PIVOTS, BLOCK), 1)
    sub = lax.broadcasted_iota(jnp.int32, (PIVOTS, BLOCK), 0)
    unit = (lane == sub).astype(jnp.float32)
    inside = lane < PIVOTS

    def step(_, held):
        rows = held[0]
        cols = [jnp.broadcast_to(rows[:, j : j + 1], (PIVOTS, BLOCK)) for j in range(PIVOTS)]
        rows = jnp.where(inside, unit, rows)
        for j in range(PIVOTS):
            inverse = 1.0 / cols[j][j : j + 1, :]
            factor = cols[j] - (sub == j).astype(jnp.float32)
            for c in range(j + 1, PIVOTS):
                cols[c] = cols[c] - factor * (cols[c][j : j + 1, :] * inverse)
            rows = rows - factor * (rows[j : j + 1, :] * inverse)
        fresh = []
        for tile in held[1:]:
            total = jnp.where(inside, 0.0, tile)
            for j in range(PIVOTS):
                total = total - tile[:, j : j + 1] * rows[j : j + 1, :]
            fresh.append(total)
        fresh.append(rows)
        return tuple(pltpu.roll(tile, BLOCK - PIVOTS, 1) for tile in fresh)

    held = tuple(block[t * PIVOTS : (t + 1) * PIVOTS, :] for t in range(tiles))
    held = lax.fori_loop(0, tiles, step, held)
    return jnp.concatenate(held, axis=0)


def factor_kernel(gram_ref, out_ref, inv_ref, work, left, right, diag, sem):
    size = gram_ref.shape[0]
    blocks = size // BLOCK
    copy = pltpu.make_async_copy(gram_ref, work, sem)
    copy.start()
    copy.wait()
    eye = (
        lax.broadcasted_iota(jnp.int32, (BLOCK, BLOCK), 0)
        == lax.broadcasted_iota(jnp.int32, (BLOCK, BLOCK), 1)
    ).astype(jnp.float32)

    def outer(k, _):
        here = pl.ds(pl.multiple_of(k * BLOCK, BLOCK), BLOCK)
        inverse = invert_block(work[here, here])
        inv_ref[here, :] = inverse
        inv_high, inv_low = split(inverse)
        diag[0:BLOCK, :] = inv_high
        diag[BLOCK : 2 * BLOCK, :] = inv_high
        diag[2 * BLOCK : 3 * BLOCK, :] = inv_low
        diag[3 * BLOCK : 4 * BLOCK, :] = inv_low
        work[here, here] = eye
        for c in range(size // CHUNK):
            cols = slice(c * CHUNK, (c + 1) * CHUNK)
            high, low = split(work[here, cols])
            right[0:BLOCK, cols] = high
            right[BLOCK : 2 * BLOCK, cols] = high
            right[2 * BLOCK : 3 * BLOCK, cols] = low
            right[3 * BLOCK : 4 * BLOCK, cols] = low

        def update(m, _):
            rows = pl.ds(pl.multiple_of(m * CHUNK, CHUNK), CHUNK)
            panel = work[rows, here]
            high, low = split(panel)
            wide = jnp.concatenate([high, low, high, low], axis=1)
            scaled = jnp.dot(wide, diag[...], preferred_element_type=jnp.float32)
            place = m * CHUNK + lax.broadcasted_iota(jnp.int32, (CHUNK, BLOCK), 0)
            later = place >= (k + 1) * BLOCK
            scaled = jnp.where(later, scaled, 0.0)
            work[rows, here] = jnp.where(later, 0.0, panel)
            high, low = split(scaled)
            wide = jnp.concatenate([high, low, high, low], axis=1)
            for c in range(size // CHUNK):
                cols = slice(c * CHUNK, (c + 1) * CHUNK)
                work[rows, cols] = work[rows, cols] - jnp.dot(
                    wide, right[:, cols], preferred_element_type=jnp.float32
                )
            return 0

        lax.fori_loop((k + 1) * BLOCK // CHUNK, size // CHUNK, update, 0)
        return 0

    lax.fori_loop(0, blocks, outer, 0)

    def clear(k, _):
        here = pl.ds(pl.multiple_of(k * BLOCK, BLOCK), BLOCK)
        for c in range(blocks):
            cols = slice(c * BLOCK, (c + 1) * BLOCK)
            work[here, cols] = jnp.where(c > k, 0.0, work[here, cols])
        return 0

    lax.fori_loop(0, blocks, clear, 0)
    copy = pltpu.make_async_copy(work, out_ref, sem)
    copy.start()
    copy.wait()


def factor(gram, interpret=False):
    size = gram.shape[0]
    return pl.pallas_call(
        factor_kernel,
        in_specs=[pl.BlockSpec(memory_space=pl.ANY)],
        out_specs=[pl.BlockSpec(memory_space=pl.ANY), pl.BlockSpec(memory_space=pltpu.VMEM)],
        out_shape=[
            jax.ShapeDtypeStruct((size, size), jnp.float32),
            jax.ShapeDtypeStruct((size, BLOCK), jnp.float32),
        ],
        scratch_shapes=[
            pltpu.VMEM((size, size), jnp.float32),
            pltpu.VMEM((16, 128), jnp.float32),
            pltpu.VMEM((4 * BLOCK, size), jnp.bfloat16),
            pltpu.VMEM((4 * BLOCK, BLOCK), jnp.bfloat16),
            pltpu.SemaphoreType.DMA,
        ],
        compiler_params=pltpu.CompilerParams(vmem_limit_bytes=40 * 2**20),
        interpret=interpret,
    )(gram)


def local(features, weights, labels, signs, samples, radius):
    highest = lax.Precision.HIGHEST
    row_count, feat_width = features.shape
    ex_count = lax.axis_size("ex")
    feat_count = lax.axis_size("feat")
    ex_index = lax.axis_index("ex")
    feat_index = lax.axis_index("feat")
    total_rows = row_count * ex_count
    sample_count = samples.shape[0]
    ridge = REG / D
    dense = features.astype(jnp.float32)
    margins = lax.psum(jnp.dot(dense, weights, precision=highest), "feat")
    probability = 1.0 / (1.0 + jnp.exp(-margins))
    curvature = probability * (1.0 - probability)
    weighted = (jnp.sqrt(curvature)[:, None] * dense).astype(jnp.bfloat16)
    signed = weighted * signs.astype(jnp.bfloat16)[:, None]
    places = ex_index * row_count + lax.iota(jnp.int32, row_count)
    odd = lax.population_count(samples[:, None] & places[None, :]) & 1
    table = (1 - 2 * odd).astype(jnp.bfloat16)
    mixed = jnp.dot(table, signed, preferred_element_type=jnp.float32)
    summed = lax.psum_scatter(mixed, "ex", scatter_dimension=0, tiled=True)
    sketch = (summed * (1.0 / math.sqrt(total_rows * sample_count))).astype(jnp.bfloat16)
    wide_sketch = lax.all_gather(sketch, "feat", axis=1, tiled=True)
    piece = lax.all_gather(wide_sketch, "ex", axis=0, tiled=True)
    gram = lax.dot_general(
        piece, piece, (((0,), (0,)), ((), ())), preferred_element_type=jnp.float32
    )
    gram = gram + ridge * jnp.eye(D, dtype=jnp.float32)
    lower, inverses = factor(gram)
    inverses = inverses.reshape(D // BLOCK, BLOCK, BLOCK)

    def apply_inverse(residual):
        middle = jnp.dot(lower, residual, precision=highest).reshape(D // BLOCK, BLOCK)
        middle = jnp.einsum("kij,kj->ki", inverses, middle, precision=highest).reshape(D)
        return jnp.dot(middle, lower, precision=highest)

    def whole(part):
        wide = jnp.zeros((D,), jnp.float32)
        return lax.dynamic_update_slice_in_dim(wide, part, feat_index * feat_width, 0)

    grad_part = jnp.dot(probability - labels.astype(jnp.float32), dense, precision=highest)
    own_rows = lax.all_to_all(weighted, "feat", split_axis=0, concat_axis=1, tiled=True)
    own_rows = own_rows.astype(jnp.float32)
    own_weights = jnp.where(ex_index == 0, weights, 0.0)
    residual = -lax.psum(whole(grad_part / total_rows + ridge * own_weights), ("ex", "feat"))

    def curve(direction):
        rows = jnp.dot(own_rows, direction, precision=highest)
        return jnp.dot(rows, own_rows, precision=highest)

    solution = jnp.zeros((D,), jnp.float32)
    solved = apply_inverse(residual)
    inner_now = jnp.dot(residual, solved)
    direction = solved
    for number in range(ITERS):
        curved = lax.psum(curve(direction), ("ex", "feat")) / total_rows + ridge * direction
        step_size = inner_now / jnp.dot(direction, curved)
        solution = solution + step_size * direction
        if number + 1 < ITERS:
            residual = residual - step_size * curved
            solved = apply_inverse(residual)
            inner_next = jnp.dot(residual, solved)
            direction = solved + inner_next / inner_now * direction
            inner_now = inner_next
    length_sq = jnp.dot(solution, solution)
    scale_step = jnp.minimum(1.0, radius[0] * math.sqrt(D) / jnp.sqrt(length_sq + 1e-06))
    own = lax.dynamic_slice_in_dim(solution, feat_index * feat_width, feat_width, 0)
    return weights + scale_step * own


def solution(mesh):
    in_specs = (P("ex", "feat"), P("feat"), P("ex"), P("ex"), P(), P())
    out_specs = P("feat")
    return jax.shard_map(local, mesh=mesh, in_specs=in_specs, out_specs=out_specs, check_vma=False)
```

```python
import functools
import math

import jax
import jax.numpy as jnp
from jax import lax
from jax.experimental import pallas as pl
from jax.experimental.pallas import tpu as pltpu
from jax.sharding import PartitionSpec as P

D = 2048
ITERS = 4
REG = 0.02
BLOCK = 128
PIVOTS = 8
CHUNK = 256


def split(value):
    high = value.astype(jnp.bfloat16)
    low = (value - high.astype(jnp.float32)).astype(jnp.bfloat16)
    return high, low


def invert_block(block):
    tiles = BLOCK // PIVOTS
    lane = lax.broadcasted_iota(jnp.int32, (PIVOTS, BLOCK), 1)
    sub = lax.broadcasted_iota(jnp.int32, (PIVOTS, BLOCK), 0)
    shape = (PIVOTS, BLOCK)
    held = [block[t * PIVOTS : (t + 1) * PIVOTS, :] for t in range(tiles)]
    for step in range(tiles):
        first = step * PIVOTS
        rows = held[step]
        inside = (lane >= first) & (lane < first + PIVOTS)
        wide = [jnp.broadcast_to(rows[:, first + j : first + j + 1], shape) for j in range(PIVOTS)]
        cell = {}
        for j in range(PIVOTS):
            for i in range(j, PIVOTS):
                cell[i, j] = jnp.broadcast_to(wide[j][i : i + 1, :], shape)
        rows = jnp.where(inside, (lane - first == sub).astype(jnp.float32), rows)
        line = [jnp.broadcast_to(rows[i : i + 1, :], shape) for i in range(PIVOTS)]
        scaled = {}
        pairs = []
        for j in range(0, PIVOTS, 2):
            a, b, d = cell[j, j], cell[j + 1, j], cell[j + 1, j + 1]
            inverse = 1.0 / (a * d - b * b)
            pairs.append((a * inverse, b * inverse, d * inverse))
            for i in range(j + 2, PIVOTS):
                one, two = cell[i, j], cell[i, j + 1]
                scaled[i, j] = one * d - two * b
                scaled[i, j + 1] = two * a - one * b
            for i in range(j + 2, PIVOTS):
                for m in range(j + 2, i + 1):
                    product = scaled[i, j] * cell[m, j] + scaled[i, j + 1] * cell[m, j + 1]
                    cell[i, m] = cell[i, m] - product * inverse
            for i in range(j + 2, PIVOTS):
                scaled[i, j] = scaled[i, j] * inverse
                scaled[i, j + 1] = scaled[i, j + 1] * inverse
                line[i] = line[i] - (scaled[i, j] * line[j] + scaled[i, j + 1] * line[j + 1])
        for j in range(PIVOTS - 2, -1, -2):
            a, b, d = pairs[j // 2]
            one = line[j] * d - line[j + 1] * b
            two = line[j + 1] * a - line[j] * b
            for i in range(j + 2, PIVOTS):
                one = one - scaled[i, j] * line[i]
                two = two - scaled[i, j + 1] * line[i]
            line[j], line[j + 1] = one, two
        for t in [(step + 1 + t) % tiles for t in range(tiles - 1)]:
            tile = held[t]
            total = jnp.where(inside, 0.0, tile)
            for j in range(PIVOTS):
                total = total - tile[:, first + j : first + j + 1] * line[j]
            held[t] = total
        rows = line[0]
        for j in range(1, PIVOTS):
            rows = jnp.where(sub == j, line[j], rows)
        held[step] = rows
    return jnp.concatenate(held, axis=0)


def factor_kernel(gram_ref, work, inv_ref, right, diag, sem):
    size = gram_ref.shape[0]
    blocks = size // BLOCK
    copy = pltpu.make_async_copy(gram_ref, work, sem)
    copy.start()
    copy.wait()
    eye = (
        lax.broadcasted_iota(jnp.int32, (BLOCK, BLOCK), 0)
        == lax.broadcasted_iota(jnp.int32, (BLOCK, BLOCK), 1)
    ).astype(jnp.float32)

    def outer(k, _):
        here = pl.ds(pl.multiple_of(k * BLOCK, BLOCK), BLOCK)
        inverse = invert_block(work[here, here])
        inv_ref[here, :] = inverse
        inv_high, inv_low = split(inverse)
        diag[0:BLOCK, :] = inv_high
        diag[BLOCK : 2 * BLOCK, :] = inv_high
        diag[2 * BLOCK : 3 * BLOCK, :] = inv_low
        diag[3 * BLOCK : 4 * BLOCK, :] = inv_low
        work[here, here] = eye
        for c in range(size // CHUNK):
            cols = slice(c * CHUNK, (c + 1) * CHUNK)
            high, low = split(work[here, cols])
            right[0:BLOCK, cols] = high
            right[BLOCK : 2 * BLOCK, cols] = high
            right[2 * BLOCK : 3 * BLOCK, cols] = low
            right[3 * BLOCK : 4 * BLOCK, cols] = low

        def update(m, _):
            rows = pl.ds(pl.multiple_of(m * CHUNK, CHUNK), CHUNK)
            panel = work[rows, here]
            high, low = split(panel)
            wide = jnp.concatenate([high, low, high, low], axis=1)
            scaled = jnp.dot(wide, diag[...], preferred_element_type=jnp.float32)
            place = m * CHUNK + lax.broadcasted_iota(jnp.int32, (CHUNK, BLOCK), 0)
            later = place >= (k + 1) * BLOCK
            scaled = jnp.where(later, scaled, 0.0)
            work[rows, here] = jnp.where(later, 0.0, panel)
            high, low = split(scaled)
            wide = jnp.concatenate([high, low, high, low], axis=1)
            for c in range(size // CHUNK):
                cols = slice(c * CHUNK, (c + 1) * CHUNK)
                work[rows, cols] = work[rows, cols] - jnp.dot(
                    wide, right[:, cols], preferred_element_type=jnp.float32
                )
            return 0

        lax.fori_loop((k + 1) * BLOCK // CHUNK, size // CHUNK, update, 0)
        return 0

    lax.fori_loop(0, blocks, outer, 0)

    def clear(k, _):
        here = pl.ds(pl.multiple_of(k * BLOCK, BLOCK), BLOCK)
        for c in range(blocks):
            cols = slice(c * BLOCK, (c + 1) * BLOCK)
            work[here, cols] = jnp.where(c > k, 0.0, work[here, cols])
        return 0

    lax.fori_loop(0, blocks, clear, 0)


VMEM = pl.BlockSpec(memory_space=pltpu.VMEM)
LIMIT = 44 * 2**20


def factor(gram, interpret=False):
    size = gram.shape[0]
    return pl.pallas_call(
        factor_kernel,
        in_specs=[pl.BlockSpec(memory_space=pl.ANY)],
        out_specs=[VMEM, VMEM],
        out_shape=[
            pltpu.VMEM((size, size), jnp.float32),
            jax.ShapeDtypeStruct((size, BLOCK), jnp.float32),
        ],
        scratch_shapes=[
            pltpu.VMEM((4 * BLOCK, size), jnp.bfloat16),
            pltpu.VMEM((4 * BLOCK, BLOCK), jnp.bfloat16),
            pltpu.SemaphoreType.DMA,
        ],
        compiler_params=pltpu.CompilerParams(vmem_limit_bytes=LIMIT),
        interpret=interpret,
    )(gram)


GROUP = 4


def apply_inverse(lower, inverses, residual):
    size = residual.shape[1]
    blocks = size // BLOCK
    eye = lax.broadcasted_iota(jnp.int32, (BLOCK, BLOCK), 0) == lax.broadcasted_iota(
        jnp.int32, (BLOCK, BLOCK), 1
    )
    total = tuple(jnp.zeros((8, BLOCK), jnp.float32) for _ in range(blocks))
    for group in range(0, blocks, GROUP):
        used = min(group + GROUP, blocks)

        def one_block(k, total):
            here = pl.ds(pl.multiple_of(k * BLOCK, BLOCK), BLOCK)
            sums = jnp.zeros((BLOCK, BLOCK), jnp.float32)
            for c in range(used):
                cols = slice(c * BLOCK, (c + 1) * BLOCK)
                sums = sums + lower[here, cols] * residual[:, cols]
            column = jnp.sum(sums, axis=1, keepdims=True)
            row = jnp.sum(inverses[here, :] * column, axis=0, keepdims=True)
            column = jnp.sum(jnp.where(eye, row, 0.0), axis=1, keepdims=True)
            fresh = list(total)
            for c in range(used):
                cols = slice(c * BLOCK, (c + 1) * BLOCK)
                product = lower[here, cols] * column
                fresh[c] = fresh[c] + jnp.sum(product.reshape(BLOCK // 8, 8, BLOCK), axis=0)
            return tuple(fresh)

        total = lax.fori_loop(group, used, one_block, total)
    return jnp.concatenate([jnp.sum(t, axis=0, keepdims=True) for t in total], axis=1)


def curve(rows_ref, direction):
    count, size = rows_ref.shape
    blocks = size // BLOCK
    high = 16

    def step(i, total):
        here = pl.ds(pl.multiple_of(i * high, high), high)
        tile = rows_ref[here, :].astype(jnp.float32)
        sums = jnp.zeros((high, BLOCK), jnp.float32)
        for c in range(blocks):
            cols = slice(c * BLOCK, (c + 1) * BLOCK)
            sums = sums + tile[:, cols] * direction[:, cols]
        column = jnp.sum(sums, axis=1, keepdims=True)
        return tuple(
            total[c] + tile[:, c * BLOCK : (c + 1) * BLOCK] * column for c in range(blocks)
        )

    total = tuple(jnp.zeros((high, BLOCK), jnp.float32) for _ in range(blocks))
    total = lax.fori_loop(0, count // high, step, total, unroll=2)
    return jnp.concatenate([jnp.sum(t, axis=0, keepdims=True) for t in total], axis=1)


def dot(left, right):
    return jnp.sum(left * right, axis=1, keepdims=True)


def first_kernel(lower, inverses, rows, residual, direction, inner, curved):
    solved = apply_inverse(lower, inverses, residual[...])
    inner[...] = dot(residual[...], solved)
    direction[...] = solved
    curved[...] = curve(rows, direction)


def next_kernel(
    total_rows, lower, inverses, rows, pieces, solution, residual, direction, inner,
    solution_out, residual_out, direction_out, inner_out, curved_out,
):
    ahead = direction[...]
    curved = jnp.sum(pieces[...], axis=0, keepdims=True) / total_rows + (REG / D) * ahead
    size = inner[...] / dot(ahead, curved)
    solution_out[...] = solution[...] + size * ahead
    left = residual[...] - size * curved
    residual_out[...] = left
    solved = apply_inverse(lower, inverses, left)
    fresh = dot(left, solved)
    inner_out[...] = fresh
    direction_out[...] = solved + fresh / inner[...] * ahead
    curved_out[...] = curve(rows, direction_out)


def last_kernel(total_rows, pieces, solution, direction, inner, radius, out):
    ahead = direction[...]
    curved = jnp.sum(pieces[...], axis=0, keepdims=True) / total_rows + (REG / D) * ahead
    size = inner[...] / dot(ahead, curved)
    full = solution[...] + size * ahead
    length_sq = dot(full, full)
    scale = jnp.minimum(1.0, radius[...] * math.sqrt(D) / jnp.sqrt(length_sq + 1e-06))
    out[...] = scale * full


def call(kernel, shapes, args):
    return pl.pallas_call(
        kernel,
        in_specs=[VMEM] * len(args),
        out_specs=[VMEM] * len(shapes),
        out_shape=[jax.ShapeDtypeStruct(shape, jnp.float32) for shape in shapes],
        compiler_params=pltpu.CompilerParams(vmem_limit_bytes=LIMIT),
    )(*args)


def exchange(value, axis):
    count = lax.axis_size(axis)
    pieces = [value]
    for mask in range(1, count):
        pieces.append(lax.ppermute(value, axis, [(s, s ^ mask) for s in range(count)]))
    return pieces


def local(features, weights, labels, signs, samples, radius):
    highest = lax.Precision.HIGHEST
    row_count, feat_width = features.shape
    ex_count = lax.axis_size("ex")
    ex_index = lax.axis_index("ex")
    feat_index = lax.axis_index("feat")
    total_rows = row_count * ex_count
    sample_count = samples.shape[0]
    ridge = REG / D
    dense = features.astype(jnp.float32)
    margins = sum(exchange(jnp.dot(dense, weights, precision=highest), "feat"))
    probability = 1.0 / (1.0 + jnp.exp(-margins))
    curvature = probability * (1.0 - probability)
    weighted = (jnp.sqrt(curvature)[:, None] * dense).astype(jnp.bfloat16)
    signed = weighted * signs.astype(jnp.bfloat16)[:, None]
    places = ex_index * row_count + lax.iota(jnp.int32, row_count)
    odd = lax.population_count(samples[:, None] & places[None, :]) & 1
    table = (1 - 2 * odd).astype(jnp.bfloat16)
    mixed = jnp.dot(table, signed, preferred_element_type=jnp.float32)
    summed = lax.psum_scatter(mixed, "ex", scatter_dimension=0, tiled=True)
    sketch = (summed * (1.0 / math.sqrt(total_rows * sample_count))).astype(jnp.bfloat16)
    wide_sketch = lax.all_gather(sketch, "feat", axis=1, tiled=True)
    piece = lax.all_gather(wide_sketch, "ex", axis=0, tiled=True)
    gram = lax.dot_general(
        piece, piece, (((0,), (0,)), ((), ())), preferred_element_type=jnp.float32
    )
    gram = gram + ridge * jnp.eye(D, dtype=jnp.float32)
    lower, inverses = factor(gram)

    grad_part = jnp.dot(probability - labels.astype(jnp.float32), dense, precision=highest)
    gradient = lax.psum(grad_part, "ex") / total_rows + ridge * weights
    own_rows = lax.all_to_all(weighted, "feat", split_axis=0, concat_axis=1, tiled=True)
    residual = -lax.all_gather(gradient, "feat", axis=0, tiled=True)[None, :]

    def across(curved):
        return jnp.concatenate(exchange(lax.psum(curved, "ex"), "feat"), axis=0)

    row, one = (1, D), (1, 1)
    direction, inner, curved = call(
        first_kernel, [row, one, row], [lower, inverses, own_rows, residual]
    )
    solution = jnp.zeros(row, jnp.float32)
    following = functools.partial(next_kernel, total_rows)
    for _ in range(ITERS - 1):
        solution, residual, direction, inner, curved = call(
            following,
            [row, row, row, one, row],
            [lower, inverses, own_rows, across(curved), solution, residual, direction, inner],
        )
    (step,) = call(
        functools.partial(last_kernel, total_rows),
        [row],
        [across(curved), solution, direction, inner, radius[None, :]],
    )
    own = lax.dynamic_slice_in_dim(step[0], feat_index * feat_width, feat_width, 0)
    return weights + own


def solution(mesh):
    in_specs = (P("ex", "feat"), P("feat"), P("ex"), P("ex"), P(), P())
    out_specs = P("feat")
    return jax.shard_map(local, mesh=mesh, in_specs=in_specs, out_specs=out_specs, check_vma=False)
```

```python
import functools
import math

import jax
import jax.numpy as jnp
from jax import lax
from jax.experimental import pallas as pl
from jax.experimental.pallas import tpu as pltpu
from jax.sharding import PartitionSpec as P

D = 2048
ITERS = 4
REG = 0.02
BLOCK = 128
PIVOTS = 8
CHUNK = 256


def split(value):
    high = value.astype(jnp.bfloat16)
    low = (value - high.astype(jnp.float32)).astype(jnp.bfloat16)
    return high, low


def invert_block(block):
    tiles = BLOCK // PIVOTS
    lane = lax.broadcasted_iota(jnp.int32, (PIVOTS, BLOCK), 1)
    sub = lax.broadcasted_iota(jnp.int32, (PIVOTS, BLOCK), 0)
    shape = (PIVOTS, BLOCK)
    held = [block[t * PIVOTS : (t + 1) * PIVOTS, :] for t in range(tiles)]
    for step in range(tiles):
        first = step * PIVOTS
        rows = held[step]
        inside = (lane >= first) & (lane < first + PIVOTS)
        wide = [jnp.broadcast_to(rows[:, first + j : first + j + 1], shape) for j in range(PIVOTS)]
        cell = {}
        for j in range(PIVOTS):
            for i in range(j, PIVOTS):
                cell[i, j] = jnp.broadcast_to(wide[j][i : i + 1, :], shape)
        rows = jnp.where(inside, (lane - first == sub).astype(jnp.float32), rows)
        line = [jnp.broadcast_to(rows[i : i + 1, :], shape) for i in range(PIVOTS)]
        scaled = {}
        pairs = []
        for j in range(0, PIVOTS, 2):
            a, b, d = cell[j, j], cell[j + 1, j], cell[j + 1, j + 1]
            inverse = 1.0 / (a * d - b * b)
            pairs.append((a * inverse, b * inverse, d * inverse))
            for i in range(j + 2, PIVOTS):
                one, two = cell[i, j], cell[i, j + 1]
                scaled[i, j] = one * d - two * b
                scaled[i, j + 1] = two * a - one * b
            for i in range(j + 2, PIVOTS):
                for m in range(j + 2, i + 1):
                    product = scaled[i, j] * cell[m, j] + scaled[i, j + 1] * cell[m, j + 1]
                    cell[i, m] = cell[i, m] - product * inverse
            for i in range(j + 2, PIVOTS):
                scaled[i, j] = scaled[i, j] * inverse
                scaled[i, j + 1] = scaled[i, j + 1] * inverse
                line[i] = line[i] - (scaled[i, j] * line[j] + scaled[i, j + 1] * line[j + 1])
        for j in range(PIVOTS - 2, -1, -2):
            a, b, d = pairs[j // 2]
            one = line[j] * d - line[j + 1] * b
            two = line[j + 1] * a - line[j] * b
            for i in range(j + 2, PIVOTS):
                one = one - scaled[i, j] * line[i]
                two = two - scaled[i, j + 1] * line[i]
            line[j], line[j + 1] = one, two
        for t in [(step + 1 + t) % tiles for t in range(tiles - 1)]:
            tile = held[t]
            total = jnp.where(inside, 0.0, tile)
            for j in range(PIVOTS):
                total = total - tile[:, first + j : first + j + 1] * line[j]
            held[t] = total
        rows = line[0]
        for j in range(1, PIVOTS):
            rows = jnp.where(sub == j, line[j], rows)
        held[step] = rows
    return jnp.concatenate(held, axis=0)


def factor_kernel(pieces, work, inv_ref, sketch, right, diag, sem):
    size = work.shape[0]
    blocks = size // BLOCK
    feat_count = pieces.shape[1]
    width = size // feat_count
    copies = [
        pltpu.make_async_copy(
            pieces.at[:, f], sketch.at[:, :, f * width : (f + 1) * width], sem.at[f]
        )
        for f in range(feat_count)
    ]
    for copy in copies:
        copy.start()
    for copy in copies:
        copy.wait()
    samples = sketch.shape[0] * sketch.shape[1]

    def gram(m, _):
        start = pl.multiple_of(m * CHUNK, CHUNK)
        here = pl.ds(start, CHUNK)
        mine = sketch[:, :, here].reshape(samples, CHUNK)
        for c in range(size // CHUNK):
            cols = slice(c * CHUNK, (c + 1) * CHUNK)
            product = lax.dot_general(
                mine,
                sketch[:, :, cols].reshape(samples, CHUNK),
                (((0,), (0,)), ((), ())),
                preferred_element_type=jnp.float32,
            )
            row = start + lax.broadcasted_iota(jnp.int32, product.shape, 0)
            col = c * CHUNK + lax.broadcasted_iota(jnp.int32, product.shape, 1)
            work[here, cols] = jnp.where(row == col, product + REG / D, product)
        return 0

    lax.fori_loop(0, size // CHUNK, gram, 0)
    eye = (
        lax.broadcasted_iota(jnp.int32, (BLOCK, BLOCK), 0)
        == lax.broadcasted_iota(jnp.int32, (BLOCK, BLOCK), 1)
    ).astype(jnp.float32)

    def outer(k, _):
        here = pl.ds(pl.multiple_of(k * BLOCK, BLOCK), BLOCK)
        inverse = invert_block(work[here, here])
        inv_ref[here, :] = inverse
        inv_high, inv_low = split(inverse)
        diag[0:BLOCK, :] = inv_high
        diag[BLOCK : 2 * BLOCK, :] = inv_high
        diag[2 * BLOCK : 3 * BLOCK, :] = inv_low
        diag[3 * BLOCK : 4 * BLOCK, :] = inv_low
        work[here, here] = eye
        for c in range(size // CHUNK):
            cols = slice(c * CHUNK, (c + 1) * CHUNK)
            high, low = split(work[here, cols])
            right[0:BLOCK, cols] = high
            right[BLOCK : 2 * BLOCK, cols] = high
            right[2 * BLOCK : 3 * BLOCK, cols] = low
            right[3 * BLOCK : 4 * BLOCK, cols] = low

        def update(m, _):
            rows = pl.ds(pl.multiple_of(m * CHUNK, CHUNK), CHUNK)
            panel = work[rows, here]
            high, low = split(panel)
            wide = jnp.concatenate([high, low, high, low], axis=1)
            scaled = jnp.dot(wide, diag[...], preferred_element_type=jnp.float32)
            place = m * CHUNK + lax.broadcasted_iota(jnp.int32, (CHUNK, BLOCK), 0)
            later = place >= (k + 1) * BLOCK
            scaled = jnp.where(later, scaled, 0.0)
            work[rows, here] = jnp.where(later, 0.0, panel)
            high, low = split(scaled)
            wide = jnp.concatenate([high, low, high, low], axis=1)
            for c in range(size // CHUNK):
                cols = slice(c * CHUNK, (c + 1) * CHUNK)
                work[rows, cols] = work[rows, cols] - jnp.dot(
                    wide, right[:, cols], preferred_element_type=jnp.float32
                )
            return 0

        lax.fori_loop((k + 1) * BLOCK // CHUNK, size // CHUNK, update, 0)
        return 0

    lax.fori_loop(0, blocks, outer, 0)

    def clear(k, _):
        here = pl.ds(pl.multiple_of(k * BLOCK, BLOCK), BLOCK)
        for c in range(blocks):
            cols = slice(c * BLOCK, (c + 1) * BLOCK)
            work[here, cols] = jnp.where(c > k, 0.0, work[here, cols])
        return 0

    lax.fori_loop(0, blocks, clear, 0)


VMEM = pl.BlockSpec(memory_space=pltpu.VMEM)


def factor(pieces, interpret=False):
    ex_count, feat_count, rows, width = pieces.shape
    size = feat_count * width
    return pl.pallas_call(
        factor_kernel,
        in_specs=[pl.BlockSpec(memory_space=pl.ANY)],
        out_specs=[VMEM, VMEM],
        out_shape=[
            pltpu.VMEM((size, size), jnp.float32),
            pltpu.VMEM((size, BLOCK), jnp.float32),
        ],
        scratch_shapes=[
            pltpu.VMEM((ex_count, rows, size), jnp.bfloat16),
            pltpu.VMEM((4 * BLOCK, size), jnp.bfloat16),
            pltpu.VMEM((4 * BLOCK, BLOCK), jnp.bfloat16),
            pltpu.SemaphoreType.DMA((feat_count,)),
        ],
        compiler_params=pltpu.CompilerParams(vmem_limit_bytes=36 * 2**20),
        interpret=interpret,
    )(pieces)


GROUP = 4


def apply_inverse(lower, inverses, residual, column):
    size = residual.shape[1]
    blocks = size // BLOCK
    eye = lax.broadcasted_iota(jnp.int32, (BLOCK, BLOCK), 0) == lax.broadcasted_iota(
        jnp.int32, (BLOCK, BLOCK), 1
    )
    for group in range(0, blocks, GROUP):
        used = group + GROUP

        def down(k, _):
            here = pl.ds(pl.multiple_of(k * BLOCK, BLOCK), BLOCK)
            sums = jnp.zeros((BLOCK, BLOCK), jnp.float32)
            for c in range(used):
                cols = slice(c * BLOCK, (c + 1) * BLOCK)
                sums = sums + lower[here, cols] * residual[:, cols]
            middle = jnp.sum(sums, axis=1, keepdims=True)
            row = jnp.sum(inverses[here, :] * middle, axis=0, keepdims=True)
            middle = jnp.sum(jnp.where(eye, row, 0.0), axis=1, keepdims=True)
            column[here, :] = jnp.broadcast_to(middle, (BLOCK, BLOCK))
            return 0

        lax.fori_loop(group, used, down, 0, unroll=True)
    total = tuple(jnp.zeros((8, BLOCK), jnp.float32) for _ in range(blocks))
    for group in range(0, blocks, GROUP):
        used = group + GROUP

        def up(t, total):
            here = pl.ds(pl.multiple_of(t * 32, 32), 32)
            middle = column[here, :]
            fresh = list(total)
            for c in range(used):
                cols = slice(c * BLOCK, (c + 1) * BLOCK)
                product = lower[here, cols] * middle
                fresh[c] = fresh[c] + jnp.sum(product.reshape(4, 8, BLOCK), axis=0)
            return tuple(fresh)

        total = lax.fori_loop(group * BLOCK // 32, used * BLOCK // 32, up, total)
    return jnp.concatenate([jnp.sum(t, axis=0, keepdims=True) for t in total], axis=1)


def curve(rows_ref, direction):
    count, size = rows_ref.shape
    blocks = size // BLOCK
    high = 16

    def step(i, total):
        here = pl.ds(pl.multiple_of(i * high, high), high)
        tile = rows_ref[here, :].astype(jnp.float32)
        sums = jnp.zeros((high, BLOCK), jnp.float32)
        for c in range(blocks):
            cols = slice(c * BLOCK, (c + 1) * BLOCK)
            sums = sums + tile[:, cols] * direction[:, cols]
        column = jnp.sum(sums, axis=1, keepdims=True)
        fresh = list(total)
        for c in range(blocks):
            product = tile[:, c * BLOCK : (c + 1) * BLOCK] * column
            fresh[c] = fresh[c] + (product[:8] + product[8:])
        return tuple(fresh)

    total = tuple(jnp.zeros((8, BLOCK), jnp.float32) for _ in range(blocks))
    total = lax.fori_loop(0, count // high, step, total, unroll=4)
    return jnp.concatenate([jnp.sum(t, axis=0, keepdims=True) for t in total], axis=1)


def dot(left, right):
    return jnp.sum(left * right, axis=1, keepdims=True)


def first_kernel(lower, inverses, rows, residual, direction, inner, curved, column):
    solved = apply_inverse(lower, inverses, residual[...], column)
    inner[...] = dot(residual[...], solved)
    direction[...] = solved
    curved[...] = curve(rows, direction)


def next_kernel(
    total_rows, lower, inverses, rows, sums, solution, residual, direction, inner,
    solution_out, residual_out, direction_out, inner_out, curved_out, column,
):
    ahead = direction[...]
    curved = sums[...] / total_rows + (REG / D) * ahead
    size = inner[...] / dot(ahead, curved)
    solution_out[...] = solution[...] + size * ahead
    left = residual[...] - size * curved
    residual_out[...] = left
    solved = apply_inverse(lower, inverses, left, column)
    fresh = dot(left, solved)
    inner_out[...] = fresh
    direction_out[...] = solved + fresh / inner[...] * ahead
    curved_out[...] = curve(rows, direction_out)


def last_kernel(total_rows, sums, solution, direction, inner, radius, out):
    ahead = direction[...]
    curved = sums[...] / total_rows + (REG / D) * ahead
    size = inner[...] / dot(ahead, curved)
    full = solution[...] + size * ahead
    length_sq = dot(full, full)
    scale = jnp.minimum(1.0, radius[...] * math.sqrt(D) / jnp.sqrt(length_sq + 1e-06))
    out[...] = scale * full


def call(kernel, shapes, args, scratch=()):
    args = list(args)
    for place, value in enumerate(args):
        if value.size >= BLOCK * D:
            args[place] = pltpu.with_memory_space_constraint(value, pltpu.VMEM)
    return pl.pallas_call(
        kernel,
        in_specs=[VMEM] * len(args),
        out_specs=[VMEM] * len(shapes),
        out_shape=[jax.ShapeDtypeStruct(shape, jnp.float32) for shape in shapes],
        scratch_shapes=scratch,
        compiler_params=pltpu.CompilerParams(vmem_limit_bytes=8 * 2**20),
    )(*args)


def exchange(value, axis):
    count = lax.axis_size(axis)
    pieces = [value]
    for mask in range(1, count):
        pieces.append(lax.ppermute(value, axis, [(s, s ^ mask) for s in range(count)]))
    return pieces


def butterfly(value):
    for axis in ("ex", "feat"):
        count = lax.axis_size(axis)
        mask = 1
        while mask < count:
            value = value + lax.ppermute(value, axis, [(s, s ^ mask) for s in range(count)])
            mask = mask * 2
    return value


def local(features, weights, labels, signs, samples, radius):
    highest = lax.Precision.HIGHEST
    row_count, feat_width = features.shape
    ex_count = lax.axis_size("ex")
    ex_index = lax.axis_index("ex")
    feat_count = lax.axis_size("feat")
    feat_index = lax.axis_index("feat")
    total_rows = row_count * ex_count
    sample_count = samples.shape[0]
    dense = features.astype(jnp.float32)
    margins = sum(exchange(jnp.dot(dense, weights, precision=highest), "feat"))
    probability = 1.0 / (1.0 + jnp.exp(-margins))
    curvature = probability * (1.0 - probability)
    weighted = (jnp.sqrt(curvature)[:, None] * dense).astype(jnp.bfloat16)
    signed = weighted * signs.astype(jnp.bfloat16)[:, None]
    places = ex_index * row_count + lax.iota(jnp.int32, row_count)
    odd = lax.population_count(samples[:, None] & places[None, :]) & 1
    table = (1 - 2 * odd).astype(jnp.bfloat16)
    mixed = jnp.dot(table, signed, preferred_element_type=jnp.float32)
    summed = lax.psum_scatter(mixed, "ex", scatter_dimension=0, tiled=True)
    sketch = (summed * (1.0 / math.sqrt(total_rows * sample_count))).astype(jnp.bfloat16)
    pieces = lax.all_gather(sketch, ("ex", "feat"), axis=0)
    lower, inverses = factor(pieces.reshape(ex_count, feat_count, *sketch.shape))

    grad_part = jnp.dot(probability - labels.astype(jnp.float32), dense, precision=highest)
    gradient = lax.psum(grad_part, "ex") / total_rows + (REG / D) * weights
    own_rows = lax.all_to_all(weighted, "feat", split_axis=0, concat_axis=1, tiled=True)
    residual = -lax.all_gather(gradient, "feat", axis=0, tiled=True)[None, :]

    row, one = (1, D), (1, 1)
    scratch = [pltpu.VMEM((D, BLOCK), jnp.float32)]
    direction, inner, curved = call(
        first_kernel, [row, one, row], [lower, inverses, own_rows, residual], scratch
    )
    solution = jnp.zeros(row, jnp.float32)
    following = functools.partial(next_kernel, total_rows)
    for _ in range(ITERS - 1):
        solution, residual, direction, inner, curved = call(
            following,
            [row, row, row, one, row],
            [lower, inverses, own_rows, butterfly(curved), solution, residual, direction, inner],
            scratch,
        )
    (step,) = call(
        functools.partial(last_kernel, total_rows),
        [row],
        [butterfly(curved), solution, direction, inner, radius[None, :]],
    )
    own = lax.dynamic_slice_in_dim(step[0], feat_index * feat_width, feat_width, 0)
    return weights + own


def solution(mesh):
    in_specs = (P("ex", "feat"), P("feat"), P("ex"), P("ex"), P(), P())
    out_specs = P("feat")
    return jax.shard_map(local, mesh=mesh, in_specs=in_specs, out_specs=out_specs, check_vma=False)
```

```python
import functools
import math

import jax
import jax.numpy as jnp
from jax import lax
from jax.experimental import pallas as pl
from jax.experimental.pallas import tpu as pltpu
from jax.sharding import PartitionSpec as P

D = 2048
ITERS = 4
REG = 0.02
BLOCK = 128
PIVOTS = 8
CHUNK = 256


def split(value):
    high = value.astype(jnp.bfloat16)
    low = (value - high.astype(jnp.float32)).astype(jnp.bfloat16)
    return high, low


def invert_block(block):
    tiles = BLOCK // PIVOTS
    lane = lax.broadcasted_iota(jnp.int32, (PIVOTS, BLOCK), 1)
    sub = lax.broadcasted_iota(jnp.int32, (PIVOTS, BLOCK), 0)
    shape = (PIVOTS, BLOCK)
    held = [block[t * PIVOTS : (t + 1) * PIVOTS, :] for t in range(tiles)]
    plain, scaled_rows = [], []
    for step in range(tiles):
        first = step * PIVOTS
        rows = held[step]
        inside = (lane >= first) & (lane < first + PIVOTS)
        before = lane < first + PIVOTS
        last = step + 1 == tiles

        def columns(tile):
            return [
                jnp.broadcast_to(tile[:, first + j : first + j + 1], shape) for j in range(PIVOTS)
            ]

        wide = columns(rows)
        cell = {}
        for j in range(PIVOTS):
            for i in range(j, PIVOTS):
                cell[i, j] = jnp.broadcast_to(wide[j][i : i + 1, :], shape)
        rows = jnp.where(inside, (lane - first == sub).astype(jnp.float32), rows)
        line = [jnp.broadcast_to(rows[i : i + 1, :], shape) for i in range(PIVOTS)]
        if not last:
            ahead = columns(held[step + 1])
            total = jnp.where(inside, 0.0, held[step + 1])
        scaled = {}
        pairs = []
        for j in range(0, PIVOTS, 2):
            a, b, d = cell[j, j], cell[j + 1, j], cell[j + 1, j + 1]
            inverse = 1.0 / (a * d - b * b)
            pairs.append((a * inverse, b * inverse, d * inverse))
            for i in range(j + 2, PIVOTS):
                one, two = cell[i, j], cell[i, j + 1]
                scaled[i, j] = one * d - two * b
                scaled[i, j + 1] = two * a - one * b
            for i in range(j + 2, PIVOTS):
                for m in range(j + 2, i + 1):
                    product = scaled[i, j] * cell[m, j] + scaled[i, j + 1] * cell[m, j + 1]
                    cell[i, m] = cell[i, m] - product * inverse
            if not last:
                one = ahead[j] * d - ahead[j + 1] * b
                two = ahead[j + 1] * a - ahead[j] * b
                for m in range(j + 2, PIVOTS):
                    product = one * cell[m, j] + two * cell[m, j + 1]
                    ahead[m] = ahead[m] - product * inverse
                total = total - (one * line[j] + two * line[j + 1]) * inverse
            for i in range(j + 2, PIVOTS):
                scaled[i, j] = scaled[i, j] * inverse
                scaled[i, j + 1] = scaled[i, j + 1] * inverse
                line[i] = line[i] - (scaled[i, j] * line[j] + scaled[i, j + 1] * line[j + 1])
        if not last:
            held[step + 1] = total
        for j in range(PIVOTS - 2, -1, -2):
            a, b, d = pairs[j // 2]
            one = line[j] * d - line[j + 1] * b
            two = line[j + 1] * a - line[j] * b
            for i in range(j + 2, PIVOTS):
                one = one - scaled[i, j] * line[i]
                two = two - scaled[i, j + 1] * line[i]
            line[j], line[j + 1] = one, two
        for t in range(step + 2, tiles):
            total = jnp.where(inside, 0.0, held[t])
            for j, column in enumerate(columns(held[t])):
                total = total - column * line[j]
            held[t] = total
        plain.append(jnp.where(before, rows, 0.0))
        rows = line[0]
        for j in range(1, PIVOTS):
            rows = jnp.where(sub == j, line[j], rows)
        scaled_rows.append(jnp.where(before, rows, 0.0))
    high, low = split(jnp.concatenate(plain, axis=0))
    left = jnp.concatenate([high, low, high, low], axis=0)
    high, low = split(jnp.concatenate(scaled_rows, axis=0))
    right = jnp.concatenate([high, high, low, low], axis=0)
    return lax.dot_general(
        left, right, (((0,), (0,)), ((), ())), preferred_element_type=jnp.float32
    )


def factor_kernel(pieces, work, inv_ref, sketch, right, diag, sem):
    size = work.shape[0]
    blocks = size // BLOCK
    feat_count = pieces.shape[1]
    width = size // feat_count
    copies = [
        pltpu.make_async_copy(
            pieces.at[:, f], sketch.at[:, :, f * width : (f + 1) * width], sem.at[f]
        )
        for f in range(feat_count)
    ]
    for copy in copies:
        copy.start()
    for copy in copies:
        copy.wait()
    samples = sketch.shape[0] * sketch.shape[1]

    def gram(m, _):
        start = pl.multiple_of(m * CHUNK, CHUNK)
        here = pl.ds(start, CHUNK)
        mine = sketch[:, :, here].reshape(samples, CHUNK)
        for c in range(size // CHUNK):
            cols = slice(c * CHUNK, (c + 1) * CHUNK)
            product = lax.dot_general(
                mine,
                sketch[:, :, cols].reshape(samples, CHUNK),
                (((0,), (0,)), ((), ())),
                preferred_element_type=jnp.float32,
            )
            row = start + lax.broadcasted_iota(jnp.int32, product.shape, 0)
            col = c * CHUNK + lax.broadcasted_iota(jnp.int32, product.shape, 1)
            work[here, cols] = jnp.where(row == col, product + REG / D, product)
        return 0

    lax.fori_loop(0, size // CHUNK, gram, 0)
    eye = (
        lax.broadcasted_iota(jnp.int32, (BLOCK, BLOCK), 0)
        == lax.broadcasted_iota(jnp.int32, (BLOCK, BLOCK), 1)
    ).astype(jnp.float32)

    def outer(k, _):
        here = pl.ds(pl.multiple_of(k * BLOCK, BLOCK), BLOCK)
        inverse = invert_block(work[here, here])
        inv_ref[here, :] = inverse
        inv_high, inv_low = split(inverse)
        diag[0:BLOCK, :] = inv_high
        diag[BLOCK : 2 * BLOCK, :] = inv_high
        diag[2 * BLOCK : 3 * BLOCK, :] = inv_low
        diag[3 * BLOCK : 4 * BLOCK, :] = inv_low
        work[here, here] = eye
        for c in range(size // CHUNK):
            cols = slice(c * CHUNK, (c + 1) * CHUNK)
            high, low = split(work[here, cols])
            right[0:BLOCK, cols] = high
            right[BLOCK : 2 * BLOCK, cols] = high
            right[2 * BLOCK : 3 * BLOCK, cols] = low
            right[3 * BLOCK : 4 * BLOCK, cols] = low

        def update(m, _):
            rows = pl.ds(pl.multiple_of(m * CHUNK, CHUNK), CHUNK)
            panel = work[rows, here]
            high, low = split(panel)
            wide = jnp.concatenate([high, low, high, low], axis=1)
            scaled = jnp.dot(wide, diag[...], preferred_element_type=jnp.float32)
            place = m * CHUNK + lax.broadcasted_iota(jnp.int32, (CHUNK, BLOCK), 0)
            later = place >= (k + 1) * BLOCK
            scaled = jnp.where(later, scaled, 0.0)
            work[rows, here] = jnp.where(later, 0.0, panel)
            high, low = split(scaled)
            wide = jnp.concatenate([high, low, high, low], axis=1)
            for c in range(size // CHUNK):
                cols = slice(c * CHUNK, (c + 1) * CHUNK)
                work[rows, cols] = work[rows, cols] - jnp.dot(
                    wide, right[:, cols], preferred_element_type=jnp.float32
                )
            return 0

        lax.fori_loop((k + 1) * BLOCK // CHUNK, size // CHUNK, update, 0)
        return 0

    lax.fori_loop(0, blocks, outer, 0)

    def clear(k, _):
        here = pl.ds(pl.multiple_of(k * BLOCK, BLOCK), BLOCK)
        for c in range(blocks):
            cols = slice(c * BLOCK, (c + 1) * BLOCK)
            work[here, cols] = jnp.where(c > k, 0.0, work[here, cols])
        return 0

    lax.fori_loop(0, blocks, clear, 0)


VMEM = pl.BlockSpec(memory_space=pltpu.VMEM)


def factor(pieces, interpret=False):
    ex_count, feat_count, rows, width = pieces.shape
    size = feat_count * width
    return pl.pallas_call(
        factor_kernel,
        in_specs=[pl.BlockSpec(memory_space=pl.ANY)],
        out_specs=[VMEM, VMEM],
        out_shape=[
            pltpu.VMEM((size, size), jnp.float32),
            pltpu.VMEM((size, BLOCK), jnp.float32),
        ],
        scratch_shapes=[
            pltpu.VMEM((ex_count, rows, size), jnp.bfloat16),
            pltpu.VMEM((4 * BLOCK, size), jnp.bfloat16),
            pltpu.VMEM((4 * BLOCK, BLOCK), jnp.bfloat16),
            pltpu.SemaphoreType.DMA((feat_count,)),
        ],
        compiler_params=pltpu.CompilerParams(vmem_limit_bytes=36 * 2**20),
        interpret=interpret,
    )(pieces)


GROUP = 4


def apply_inverse(lower, inverses, residual, column):
    size = residual.shape[1]
    blocks = size // BLOCK
    eye = lax.broadcasted_iota(jnp.int32, (BLOCK, BLOCK), 0) == lax.broadcasted_iota(
        jnp.int32, (BLOCK, BLOCK), 1
    )
    for group in range(0, blocks, GROUP):
        used = group + GROUP

        def down(k, _):
            here = pl.ds(pl.multiple_of(k * BLOCK, BLOCK), BLOCK)
            sums = jnp.zeros((BLOCK, BLOCK), jnp.float32)
            for c in range(used):
                cols = slice(c * BLOCK, (c + 1) * BLOCK)
                sums = sums + lower[here, cols] * residual[:, cols]
            middle = jnp.sum(sums, axis=1, keepdims=True)
            row = jnp.sum(inverses[here, :] * middle, axis=0, keepdims=True)
            middle = jnp.sum(jnp.where(eye, row, 0.0), axis=1, keepdims=True)
            column[here, :] = jnp.broadcast_to(middle, (BLOCK, BLOCK))
            return 0

        lax.fori_loop(group, used, down, 0, unroll=True)
    total = tuple(jnp.zeros((8, BLOCK), jnp.float32) for _ in range(blocks))
    for group in range(0, blocks, GROUP):
        used = group + GROUP

        def up(t, total):
            here = pl.ds(pl.multiple_of(t * 32, 32), 32)
            middle = column[here, :]
            fresh = list(total)
            for c in range(used):
                cols = slice(c * BLOCK, (c + 1) * BLOCK)
                product = lower[here, cols] * middle
                fresh[c] = fresh[c] + jnp.sum(product.reshape(4, 8, BLOCK), axis=0)
            return tuple(fresh)

        total = lax.fori_loop(group * BLOCK // 32, used * BLOCK // 32, up, total)
    return jnp.concatenate([jnp.sum(t, axis=0, keepdims=True) for t in total], axis=1)


def curve(rows_ref, direction):
    count, size = rows_ref.shape
    blocks = size // BLOCK
    high = 16

    def step(i, total):
        here = pl.ds(pl.multiple_of(i * high, high), high)
        tile = rows_ref[here, :].astype(jnp.float32)
        sums = jnp.zeros((high, BLOCK), jnp.float32)
        for c in range(blocks):
            cols = slice(c * BLOCK, (c + 1) * BLOCK)
            sums = sums + tile[:, cols] * direction[:, cols]
        column = jnp.sum(sums, axis=1, keepdims=True)
        fresh = list(total)
        for c in range(blocks):
            product = tile[:, c * BLOCK : (c + 1) * BLOCK] * column
            fresh[c] = fresh[c] + (product[:8] + product[8:])
        return tuple(fresh)

    total = tuple(jnp.zeros((8, BLOCK), jnp.float32) for _ in range(blocks))
    total = lax.fori_loop(0, count // high, step, total, unroll=4)
    return jnp.concatenate([jnp.sum(t, axis=0, keepdims=True) for t in total], axis=1)


def dot(left, right):
    return jnp.sum(left * right, axis=1, keepdims=True)


def first_kernel(lower, inverses, rows, residual, direction, inner, curved, column):
    solved = apply_inverse(lower, inverses, residual[...], column)
    inner[...] = dot(residual[...], solved)
    direction[...] = solved
    curved[...] = curve(rows, direction)


def next_kernel(
    total_rows, lower, inverses, rows, sums, solution, residual, direction, inner,
    solution_out, residual_out, direction_out, inner_out, curved_out, column,
):
    ahead = direction[...]
    curved = sums[...] / total_rows + (REG / D) * ahead
    size = inner[...] / dot(ahead, curved)
    solution_out[...] = solution[...] + size * ahead
    left = residual[...] - size * curved
    residual_out[...] = left
    solved = apply_inverse(lower, inverses, left, column)
    fresh = dot(left, solved)
    inner_out[...] = fresh
    direction_out[...] = solved + fresh / inner[...] * ahead
    curved_out[...] = curve(rows, direction_out)


def last_kernel(total_rows, sums, solution, direction, inner, radius, out):
    ahead = direction[...]
    curved = sums[...] / total_rows + (REG / D) * ahead
    size = inner[...] / dot(ahead, curved)
    full = solution[...] + size * ahead
    length_sq = dot(full, full)
    scale = jnp.minimum(1.0, radius[...] * math.sqrt(D) / jnp.sqrt(length_sq + 1e-06))
    out[...] = scale * full


def call(kernel, shapes, args, scratch=()):
    args = list(args)
    for place, value in enumerate(args):
        if value.size >= BLOCK * D:
            args[place] = pltpu.with_memory_space_constraint(value, pltpu.VMEM)
    return pl.pallas_call(
        kernel,
        in_specs=[VMEM] * len(args),
        out_specs=[VMEM] * len(shapes),
        out_shape=[jax.ShapeDtypeStruct(shape, jnp.float32) for shape in shapes],
        scratch_shapes=scratch,
        compiler_params=pltpu.CompilerParams(vmem_limit_bytes=8 * 2**20),
    )(*args)


def exchange(value, axis):
    count = lax.axis_size(axis)
    pieces = [value]
    for mask in range(1, count):
        pieces.append(lax.ppermute(value, axis, [(s, s ^ mask) for s in range(count)]))
    return pieces


def swap(value, axis, bit):
    mask = 2**bit
    return lax.ppermute(value, axis, [(s, s ^ mask) for s in range(lax.axis_size(axis))])


def bit_places(order):
    places = [0]
    for bit in reversed(order):
        places = places + [place | 2**bit for place in places]
    return places


def sampled_mix(samples, places, signed):
    count = lax.axis_size("ex")
    grid = samples.reshape(count * 2, -1)
    upward = list(range(1, count.bit_length() - 1))
    downward = upward[::-1]
    wanted = [(q, 0) for q in bit_places(upward)] + [(q, 1) for q in bit_places(downward)]
    numbers = jnp.array([[q ^ 1, half] for q, half in wanted] + [[q, half] for q, half in wanted])
    rows = grid[(numbers[:, 0] ^ lax.axis_index("ex")) * 2 + numbers[:, 1]].reshape(2, -1)

    def mix(chosen):
        odd = lax.population_count(chosen[:, None] & places[None, :]) & 1
        table = (1 - 2 * odd).astype(jnp.bfloat16)
        return jnp.dot(table, signed, preferred_element_type=jnp.float32)

    total = swap(mix(rows[0]), "ex", 0) + mix(rows[1])
    parts = list(jnp.split(total, 2))
    for bits in zip(upward, downward):
        halves = [jnp.split(part, 2) for part in parts]
        got = [swap(half[1], "ex", bit) for half, bit in zip(halves, bits)]
        parts = [half[0] + other for half, other in zip(halves, got)]
    return jnp.concatenate(parts)


def butterfly(value):
    for axis in ("ex", "feat"):
        count = lax.axis_size(axis)
        mask = 1
        while mask < count:
            value = value + lax.ppermute(value, axis, [(s, s ^ mask) for s in range(count)])
            mask = mask * 2
    return value


def local(features, weights, labels, signs, samples, radius):
    highest = lax.Precision.HIGHEST
    row_count, feat_width = features.shape
    ex_count = lax.axis_size("ex")
    ex_index = lax.axis_index("ex")
    feat_count = lax.axis_size("feat")
    feat_index = lax.axis_index("feat")
    total_rows = row_count * ex_count
    sample_count = samples.shape[0]
    dense = features.astype(jnp.float32)
    margins = sum(exchange(jnp.dot(dense, weights, precision=highest), "feat"))
    probability = 1.0 / (1.0 + jnp.exp(-margins))
    curvature = probability * (1.0 - probability)
    weighted = (jnp.sqrt(curvature)[:, None] * dense).astype(jnp.bfloat16)
    signed = weighted * signs.astype(jnp.bfloat16)[:, None]
    places = ex_index * row_count + lax.iota(jnp.int32, row_count)
    total = sampled_mix(samples, places, signed)
    sketch = (total * (1.0 / math.sqrt(total_rows * sample_count))).astype(jnp.bfloat16)
    pieces = lax.all_gather(lax.all_gather(sketch, "feat", axis=0), "ex", axis=0)
    lower, inverses = factor(pieces)

    grad_part = jnp.dot(probability - labels.astype(jnp.float32), dense, precision=highest)
    gradient = lax.psum(grad_part, "ex") / total_rows + (REG / D) * weights
    own_rows = lax.all_to_all(weighted, "feat", split_axis=0, concat_axis=1, tiled=True)
    residual = -lax.all_gather(gradient, "feat", axis=0, tiled=True)[None, :]

    row, one = (1, D), (1, 1)
    scratch = [pltpu.VMEM((D, BLOCK), jnp.float32)]
    direction, inner, curved = call(
        first_kernel, [row, one, row], [lower, inverses, own_rows, residual], scratch
    )
    solution = jnp.zeros(row, jnp.float32)
    following = functools.partial(next_kernel, total_rows)
    for _ in range(ITERS - 1):
        solution, residual, direction, inner, curved = call(
            following,
            [row, row, row, one, row],
            [lower, inverses, own_rows, butterfly(curved), solution, residual, direction, inner],
            scratch,
        )
    (step,) = call(
        functools.partial(last_kernel, total_rows),
        [row],
        [butterfly(curved), solution, direction, inner, radius[None, :]],
    )
    own = lax.dynamic_slice_in_dim(step[0], feat_index * feat_width, feat_width, 0)
    return weights + own


def solution(mesh):
    in_specs = (P("ex", "feat"), P("feat"), P("ex"), P("ex"), P(), P())
    out_specs = P("feat")
    return jax.shard_map(local, mesh=mesh, in_specs=in_specs, out_specs=out_specs, check_vma=False)
```

```python
import functools
import math

import jax
import jax.numpy as jnp
from jax import lax
from jax.experimental import pallas as pl
from jax.experimental.pallas import tpu as pltpu
from jax.sharding import PartitionSpec as P

D = 2048
ITERS = 4
REG = 0.02
BLOCK = 128
PIVOTS = 8
CHUNK = 256
GROUP = 4


def split(value):
    high = value.astype(jnp.bfloat16)
    low = (value - high.astype(jnp.float32)).astype(jnp.bfloat16)
    return high, low


def invert_block(block, pieces=()):
    tiles = BLOCK // PIVOTS
    lane = lax.broadcasted_iota(jnp.int32, (PIVOTS, BLOCK), 1)
    sub = lax.broadcasted_iota(jnp.int32, (PIVOTS, BLOCK), 0)
    shape = (PIVOTS, BLOCK)
    held = [block[t * PIVOTS : (t + 1) * PIVOTS, :] for t in range(tiles)]
    plain, scaled_rows = [], []
    for step in range(tiles):
        first = step * PIVOTS
        rows = held[step]
        inside = (lane >= first) & (lane < first + PIVOTS)
        before = lane < first + PIVOTS
        last = step + 1 == tiles

        def columns(tile):
            return [
                jnp.broadcast_to(tile[:, first + j : first + j + 1], shape) for j in range(PIVOTS)
            ]

        wide = columns(rows)
        cell = {}
        for j in range(PIVOTS):
            for i in range(j, PIVOTS):
                cell[i, j] = jnp.broadcast_to(wide[j][i : i + 1, :], shape)
        rows = jnp.where(inside, (lane - first == sub).astype(jnp.float32), rows)
        line = [jnp.broadcast_to(rows[i : i + 1, :], shape) for i in range(PIVOTS)]
        if not last:
            ahead = columns(held[step + 1])
            total = jnp.where(inside, 0.0, held[step + 1])
        scaled = {}
        pairs = []
        for j in range(0, PIVOTS, 2):
            a, b, d = cell[j, j], cell[j + 1, j], cell[j + 1, j + 1]
            inverse = 1.0 / (a * d - b * b)
            pairs.append((a * inverse, b * inverse, d * inverse))
            for i in range(j + 2, PIVOTS):
                one, two = cell[i, j], cell[i, j + 1]
                scaled[i, j] = one * d - two * b
                scaled[i, j + 1] = two * a - one * b
            for i in range(j + 2, PIVOTS):
                for m in range(j + 2, i + 1):
                    product = scaled[i, j] * cell[m, j] + scaled[i, j + 1] * cell[m, j + 1]
                    cell[i, m] = cell[i, m] - product * inverse
            if not last:
                one = ahead[j] * d - ahead[j + 1] * b
                two = ahead[j + 1] * a - ahead[j] * b
                for m in range(j + 2, PIVOTS):
                    product = one * cell[m, j] + two * cell[m, j + 1]
                    ahead[m] = ahead[m] - product * inverse
                total = total - (one * line[j] + two * line[j + 1]) * inverse
            for i in range(j + 2, PIVOTS):
                scaled[i, j] = scaled[i, j] * inverse
                scaled[i, j + 1] = scaled[i, j + 1] * inverse
                line[i] = line[i] - (scaled[i, j] * line[j] + scaled[i, j + 1] * line[j + 1])
        if not last:
            held[step + 1] = total
        for j in range(PIVOTS - 2, -1, -2):
            a, b, d = pairs[j // 2]
            one = line[j] * d - line[j + 1] * b
            two = line[j + 1] * a - line[j] * b
            for i in range(j + 2, PIVOTS):
                one = one - scaled[i, j] * line[i]
                two = two - scaled[i, j + 1] * line[i]
            line[j], line[j + 1] = one, two
        for t in range(step + 2, tiles):
            total = jnp.where(inside, 0.0, held[t])
            for j, column in enumerate(columns(held[t])):
                total = total - column * line[j]
            held[t] = total
        plain.append(jnp.where(before, rows, 0.0))
        rows = line[0]
        for j in range(1, PIVOTS):
            rows = jnp.where(sub == j, line[j], rows)
        scaled_rows.append(jnp.where(before, rows, 0.0))
        for piece in pieces[step * len(pieces) // tiles : (step + 1) * len(pieces) // tiles]:
            piece()
    high, low = split(jnp.concatenate(plain, axis=0))
    left = jnp.concatenate([high, low, high, low], axis=0)
    high, low = split(jnp.concatenate(scaled_rows, axis=0))
    right = jnp.concatenate([high, high, low, low], axis=0)
    return lax.dot_general(
        left, right, (((0,), (0,)), ((), ())), preferred_element_type=jnp.float32
    )


def factor_kernel(pieces, work, inv_ref, sketch, right, left, sem):
    size = work.shape[0]
    blocks = size // BLOCK
    feat_count = pieces.shape[1]
    width = size // feat_count
    copies = [
        pltpu.make_async_copy(
            pieces.at[:, f], sketch.at[:, :, f * width : (f + 1) * width], sem.at[f]
        )
        for f in range(feat_count)
    ]
    for copy in copies:
        copy.start()
    for copy in copies:
        copy.wait()
    samples = sketch.shape[0] * sketch.shape[1]

    chunks = size // CHUNK

    def chunk(c):
        return slice(c * CHUNK, (c + 1) * CHUNK)

    def gram(m, _):
        start = pl.multiple_of(m * CHUNK, CHUNK)
        here = pl.ds(start, CHUNK)
        for c in range(chunks):

            @pl.when(c >= m)
            def _():
                product = lax.dot_general(
                    sketch[:, :, here].reshape(samples, CHUNK),
                    sketch[:, :, chunk(c)].reshape(samples, CHUNK),
                    (((0,), (0,)), ((), ())),
                    preferred_element_type=jnp.float32,
                )
                row = start + lax.broadcasted_iota(jnp.int32, product.shape, 0)
                col = c * CHUNK + lax.broadcasted_iota(jnp.int32, product.shape, 1)
                work[here, chunk(c)] = jnp.where(row == col, product + REG / D, product)

        return 0

    lax.fori_loop(0, chunks, gram, 0)
    eye = (
        lax.broadcasted_iota(jnp.int32, (BLOCK, BLOCK), 0)
        == lax.broadcasted_iota(jnp.int32, (BLOCK, BLOCK), 1)
    ).astype(jnp.float32)

    def prepare(k, inverse, lowest):
        here = pl.ds(pl.multiple_of(k * BLOCK, BLOCK), BLOCK)
        inv_ref[here, :] = inverse
        high, low = split(inverse)
        diag = jnp.concatenate([high, high, low, low], axis=0)
        work[here, here] = eye
        for c in range(chunks):
            panel = work[here, chunk(c)]
            high, low = split(panel)
            right[0:BLOCK, chunk(c)] = high
            right[BLOCK : 2 * BLOCK, chunk(c)] = high
            right[2 * BLOCK : 3 * BLOCK, chunk(c)] = low
            right[3 * BLOCK : 4 * BLOCK, chunk(c)] = low
            if c >= lowest:
                high, low = split(panel.T)
                wide = jnp.concatenate([high, low, high, low], axis=1)
                scaled = jnp.dot(wide, diag, preferred_element_type=jnp.float32)
                place = c * CHUNK + lax.broadcasted_iota(jnp.int32, (CHUNK, BLOCK), 0)
                high, low = split(jnp.where(place >= (k + 1) * BLOCK, scaled, 0.0))
                left[chunk(c), :] = jnp.concatenate([high, low, high, low], axis=1)

    def update(k, m, c, lowest):
        product = jnp.dot(
            left[chunk(m), :], right[:, chunk(c)], preferred_element_type=jnp.float32
        )
        value = work[chunk(m), chunk(c)]
        if lowest <= c < lowest + GROUP * BLOCK // CHUNK:
            row = m * CHUNK + lax.broadcasted_iota(jnp.int32, value.shape, 0)
            col = c * CHUNK + lax.broadcasted_iota(jnp.int32, value.shape, 1)
            fresh = (col >= k * BLOCK) & (col < (k + 1) * BLOCK) & (row >= (k + 1) * BLOCK)
            value = jnp.where(fresh, 0.0, value)
        work[chunk(m), chunk(c)] = value - product

    prepare(0, invert_block(work[0:BLOCK, 0:BLOCK]), 0)
    for first in range(0, blocks, GROUP):
        lowest = first * BLOCK // CHUNK
        settled = lowest + GROUP * BLOCK // CHUNK
        wanted = [
            (m, c) for m in range(lowest, chunks) for c in range(chunks) if c < settled or c >= m
        ]

        def outer(k, _):
            following = pl.ds(pl.multiple_of((k + 1) * BLOCK, BLOCK), BLOCK)
            block = work[following, following] - jnp.dot(
                left[following, :], right[:, following], preferred_element_type=jnp.float32
            )
            inverse = invert_block(
                block, [functools.partial(update, k, m, c, lowest) for m, c in wanted]
            )
            prepare(k + 1, inverse, lowest)
            return 0

        lax.fori_loop(first, min(first + GROUP, blocks - 1), outer, 0)
    for k in range(blocks):
        last = k // GROUP * GROUP + GROUP
        if k + 1 < last:
            work[k * BLOCK : (k + 1) * BLOCK, (k + 1) * BLOCK : last * BLOCK] = jnp.zeros(
                (BLOCK, (last - k - 1) * BLOCK), jnp.float32
            )


VMEM = pl.BlockSpec(memory_space=pltpu.VMEM)


def factor(pieces, interpret=False):
    ex_count, feat_count, rows, width = pieces.shape
    size = feat_count * width
    return pl.pallas_call(
        factor_kernel,
        in_specs=[pl.BlockSpec(memory_space=pl.ANY)],
        out_specs=[VMEM, VMEM],
        out_shape=[
            pltpu.VMEM((size, size), jnp.float32),
            pltpu.VMEM((size, BLOCK), jnp.float32),
        ],
        scratch_shapes=[
            pltpu.VMEM((ex_count, rows, size), jnp.bfloat16),
            pltpu.VMEM((4 * BLOCK, size), jnp.bfloat16),
            pltpu.VMEM((size, 4 * BLOCK), jnp.bfloat16),
            pltpu.SemaphoreType.DMA((feat_count,)),
        ],
        compiler_params=pltpu.CompilerParams(vmem_limit_bytes=36 * 2**20),
        interpret=interpret,
    )(pieces)


def apply_inverse(lower, inverses, residual, column):
    size = residual.shape[1]
    blocks = size // BLOCK
    eye = lax.broadcasted_iota(jnp.int32, (BLOCK, BLOCK), 0) == lax.broadcasted_iota(
        jnp.int32, (BLOCK, BLOCK), 1
    )
    for group in range(0, blocks, GROUP):
        used = group + GROUP

        def down(k, _):
            here = pl.ds(pl.multiple_of(k * BLOCK, BLOCK), BLOCK)
            sums = jnp.zeros((BLOCK, BLOCK), jnp.float32)
            for c in range(used):
                cols = slice(c * BLOCK, (c + 1) * BLOCK)
                sums = sums + lower[here, cols] * residual[:, cols]
            middle = jnp.sum(sums, axis=1, keepdims=True)
            row = jnp.sum(inverses[here, :] * middle, axis=0, keepdims=True)
            middle = jnp.sum(jnp.where(eye, row, 0.0), axis=1, keepdims=True)
            column[here, :] = jnp.broadcast_to(middle, (BLOCK, BLOCK))
            return 0

        lax.fori_loop(group, used, down, 0, unroll=True)
    total = tuple(jnp.zeros((8, BLOCK), jnp.float32) for _ in range(blocks))
    for group in range(0, blocks, GROUP):
        used = group + GROUP

        def up(t, total):
            here = pl.ds(pl.multiple_of(t * 32, 32), 32)
            middle = column[here, :]
            fresh = list(total)
            for c in range(used):
                cols = slice(c * BLOCK, (c + 1) * BLOCK)
                product = lower[here, cols] * middle
                fresh[c] = fresh[c] + jnp.sum(product.reshape(4, 8, BLOCK), axis=0)
            return tuple(fresh)

        total = lax.fori_loop(group * BLOCK // 32, used * BLOCK // 32, up, total)
    return jnp.concatenate([jnp.sum(t, axis=0, keepdims=True) for t in total], axis=1)


def curve(rows_ref, direction):
    count, size = rows_ref.shape
    blocks = size // BLOCK
    high = 16

    def step(i, total):
        here = pl.ds(pl.multiple_of(i * high, high), high)
        tile = rows_ref[here, :].astype(jnp.float32)
        sums = jnp.zeros((high, BLOCK), jnp.float32)
        for c in range(blocks):
            cols = slice(c * BLOCK, (c + 1) * BLOCK)
            sums = sums + tile[:, cols] * direction[:, cols]
        column = jnp.sum(sums, axis=1, keepdims=True)
        fresh = list(total)
        for c in range(blocks):
            product = tile[:, c * BLOCK : (c + 1) * BLOCK] * column
            fresh[c] = fresh[c] + (product[:8] + product[8:])
        return tuple(fresh)

    total = tuple(jnp.zeros((8, BLOCK), jnp.float32) for _ in range(blocks))
    total = lax.fori_loop(0, count // high, step, total, unroll=4)
    return jnp.concatenate([jnp.sum(t, axis=0, keepdims=True) for t in total], axis=1)


def dot(left, right):
    return jnp.sum(left * right, axis=1, keepdims=True)


def first_kernel(lower, inverses, rows, residual, direction, inner, curved, column):
    solved = apply_inverse(lower, inverses, residual[...], column)
    inner[...] = dot(residual[...], solved)
    direction[...] = solved
    curved[...] = curve(rows, direction)


def next_kernel(
    total_rows, lower, inverses, rows, sums, solution, residual, direction, inner,
    solution_out, residual_out, direction_out, inner_out, curved_out, column,
):
    ahead = direction[...]
    curved = sums[...] / total_rows + (REG / D) * ahead
    size = inner[...] / dot(ahead, curved)
    solution_out[...] = solution[...] + size * ahead
    left = residual[...] - size * curved
    residual_out[...] = left
    solved = apply_inverse(lower, inverses, left, column)
    fresh = dot(left, solved)
    inner_out[...] = fresh
    direction_out[...] = solved + fresh / inner[...] * ahead
    curved_out[...] = curve(rows, direction_out)


def last_kernel(total_rows, sums, solution, direction, inner, radius, out):
    ahead = direction[...]
    curved = sums[...] / total_rows + (REG / D) * ahead
    size = inner[...] / dot(ahead, curved)
    full = solution[...] + size * ahead
    length_sq = dot(full, full)
    scale = jnp.minimum(1.0, radius[...] * math.sqrt(D) / jnp.sqrt(length_sq + 1e-06))
    out[...] = scale * full


def call(kernel, shapes, args, scratch=()):
    args = list(args)
    for place, value in enumerate(args):
        if value.size >= BLOCK * D:
            args[place] = pltpu.with_memory_space_constraint(value, pltpu.VMEM)
    return pl.pallas_call(
        kernel,
        in_specs=[VMEM] * len(args),
        out_specs=[VMEM] * len(shapes),
        out_shape=[jax.ShapeDtypeStruct(shape, jnp.float32) for shape in shapes],
        scratch_shapes=scratch,
        compiler_params=pltpu.CompilerParams(vmem_limit_bytes=8 * 2**20),
    )(*args)


def exchange(value, axis):
    count = lax.axis_size(axis)
    pieces = [value]
    for mask in range(1, count):
        pieces.append(lax.ppermute(value, axis, [(s, s ^ mask) for s in range(count)]))
    return pieces


def swap(value, axis, bit):
    mask = 2**bit
    return lax.ppermute(value, axis, [(s, s ^ mask) for s in range(lax.axis_size(axis))])


def bit_places(order):
    places = [0]
    for bit in reversed(order):
        places = places + [place | 2**bit for place in places]
    return places


def sampled_mix(samples, places, signed):
    count = lax.axis_size("ex")
    grid = samples.reshape(count * 2, -1)
    upward = list(range(1, count.bit_length() - 1))
    downward = upward[::-1]
    wanted = [(q, 0) for q in bit_places(upward)] + [(q, 1) for q in bit_places(downward)]
    numbers = jnp.array([[q ^ 1, half] for q, half in wanted] + [[q, half] for q, half in wanted])
    rows = grid[(numbers[:, 0] ^ lax.axis_index("ex")) * 2 + numbers[:, 1]].reshape(2, -1)

    def mix(chosen):
        odd = lax.population_count(chosen[:, None] & places[None, :]) & 1
        table = (1 - 2 * odd).astype(jnp.bfloat16)
        return jnp.dot(table, signed, preferred_element_type=jnp.float32)

    total = swap(mix(rows[0]), "ex", 0) + mix(rows[1])
    parts = list(jnp.split(total, 2))
    for bits in zip(upward, downward):
        halves = [jnp.split(part, 2) for part in parts]
        got = [swap(half[1], "ex", bit) for half, bit in zip(halves, bits)]
        got = lax.optimization_barrier(got)
        parts = [half[0] + other for half, other in zip(halves, got)]
    return jnp.concatenate(parts)


def butterfly(value):
    for axis in ("ex", "feat"):
        count = lax.axis_size(axis)
        mask = 1
        while mask < count:
            value = value + lax.ppermute(value, axis, [(s, s ^ mask) for s in range(count)])
            mask = mask * 2
    return value


def local(features, weights, labels, signs, samples, radius):
    highest = lax.Precision.HIGHEST
    row_count, feat_width = features.shape
    ex_count = lax.axis_size("ex")
    ex_index = lax.axis_index("ex")
    feat_count = lax.axis_size("feat")
    feat_index = lax.axis_index("feat")
    total_rows = row_count * ex_count
    sample_count = samples.shape[0]
    dense = features.astype(jnp.float32)
    margins = sum(exchange(jnp.dot(dense, weights, precision=highest), "feat"))
    probability = 1.0 / (1.0 + jnp.exp(-margins))
    curvature = probability * (1.0 - probability)
    weighted = (jnp.sqrt(curvature)[:, None] * dense).astype(jnp.bfloat16)
    signed = weighted * signs.astype(jnp.bfloat16)[:, None]
    places = ex_index * row_count + lax.iota(jnp.int32, row_count)
    total = sampled_mix(samples, places, signed)
    sketch = (total * (1.0 / math.sqrt(total_rows * sample_count))).astype(jnp.bfloat16)
    pieces = lax.all_gather(lax.all_gather(sketch, "feat", axis=0), "ex", axis=0)
    lower, inverses = factor(pieces)

    grad_part = jnp.dot(probability - labels.astype(jnp.float32), dense, precision=highest)
    gradient = lax.psum(grad_part, "ex") / total_rows + (REG / D) * weights
    own_rows = lax.all_to_all(weighted, "feat", split_axis=0, concat_axis=1, tiled=True)
    residual = -lax.all_gather(gradient, "feat", axis=0, tiled=True)[None, :]

    row, one = (1, D), (1, 1)
    scratch = [pltpu.VMEM((D, BLOCK), jnp.float32)]
    direction, inner, curved = call(
        first_kernel, [row, one, row], [lower, inverses, own_rows, residual], scratch
    )
    solution = jnp.zeros(row, jnp.float32)
    following = functools.partial(next_kernel, total_rows)
    for _ in range(ITERS - 1):
        solution, residual, direction, inner, curved = call(
            following,
            [row, row, row, one, row],
            [lower, inverses, own_rows, butterfly(curved), solution, residual, direction, inner],
            scratch,
        )
    (step,) = call(
        functools.partial(last_kernel, total_rows),
        [row],
        [butterfly(curved), solution, direction, inner, radius[None, :]],
    )
    own = lax.dynamic_slice_in_dim(step[0], feat_index * feat_width, feat_width, 0)
    return weights + own


def solution(mesh):
    in_specs = (P("ex", "feat"), P("feat"), P("ex"), P("ex"), P(), P())
    out_specs = P("feat")
    return jax.shard_map(local, mesh=mesh, in_specs=in_specs, out_specs=out_specs, check_vma=False)
```

```python
import functools
import math

import jax
import jax.numpy as jnp
from jax import lax
from jax.experimental import pallas as pl
from jax.experimental.pallas import tpu as pltpu
from jax.sharding import PartitionSpec as P

D = 2048
ITERS = 4
REG = 0.02
BLOCK = 128
PIVOTS = 8
CHUNK = 256
GROUP = 4


def split(value):
    high = value.astype(jnp.bfloat16)
    low = (value - high.astype(jnp.float32)).astype(jnp.bfloat16)
    return high, low


def reciprocal(value):
    guess = pl.reciprocal(value, approx=True)
    guess = guess * (2.0 - value * guess)
    return guess * (2.0 - value * guess)


def invert_block(block, pieces=()):
    tiles = BLOCK // PIVOTS
    lane = lax.broadcasted_iota(jnp.int32, (PIVOTS, BLOCK), 1)
    sub = lax.broadcasted_iota(jnp.int32, (PIVOTS, BLOCK), 0)
    shape = (PIVOTS, BLOCK)
    held = [block[t * PIVOTS : (t + 1) * PIVOTS, :] for t in range(tiles)]
    plain, scaled_rows = [], []
    for step in range(tiles):
        first = step * PIVOTS
        rows = held[step]
        inside = (lane >= first) & (lane < first + PIVOTS)
        before = lane < first + PIVOTS
        last = step + 1 == tiles

        def columns(tile):
            return [
                jnp.broadcast_to(tile[:, first + j : first + j + 1], shape) for j in range(PIVOTS)
            ]

        wide = columns(rows)
        cell = {}
        for j in range(PIVOTS):
            for i in range(j, PIVOTS):
                cell[i, j] = jnp.broadcast_to(wide[j][i : i + 1, :], shape)
        rows = jnp.where(inside, (lane - first == sub).astype(jnp.float32), rows)
        line = [jnp.broadcast_to(rows[i : i + 1, :], shape) for i in range(PIVOTS)]
        if not last:
            ahead = columns(held[step + 1])
            total = jnp.where(inside, 0.0, held[step + 1])
        scaled = {}
        pairs = []
        for j in range(0, PIVOTS, 2):
            a, b, d = cell[j, j], cell[j + 1, j], cell[j + 1, j + 1]
            inverse = reciprocal(a * d - b * b)
            pairs.append((a * inverse, b * inverse, d * inverse))
            for i in range(j + 2, PIVOTS):
                one, two = cell[i, j], cell[i, j + 1]
                scaled[i, j] = one * d - two * b
                scaled[i, j + 1] = two * a - one * b
            for i in range(j + 2, PIVOTS):
                for m in range(j + 2, i + 1):
                    product = scaled[i, j] * cell[m, j] + scaled[i, j + 1] * cell[m, j + 1]
                    cell[i, m] = cell[i, m] - product * inverse
            if not last:
                one = ahead[j] * d - ahead[j + 1] * b
                two = ahead[j + 1] * a - ahead[j] * b
                for m in range(j + 2, PIVOTS):
                    product = one * cell[m, j] + two * cell[m, j + 1]
                    ahead[m] = ahead[m] - product * inverse
                total = total - (one * line[j] + two * line[j + 1]) * inverse
            for i in range(j + 2, PIVOTS):
                scaled[i, j] = scaled[i, j] * inverse
                scaled[i, j + 1] = scaled[i, j + 1] * inverse
                line[i] = line[i] - (scaled[i, j] * line[j] + scaled[i, j + 1] * line[j + 1])
        if not last:
            held[step + 1] = total
        for j in range(PIVOTS - 2, -1, -2):
            a, b, d = pairs[j // 2]
            one = line[j] * d - line[j + 1] * b
            two = line[j + 1] * a - line[j] * b
            for i in range(j + 2, PIVOTS):
                one = one - scaled[i, j] * line[i]
                two = two - scaled[i, j + 1] * line[i]
            line[j], line[j + 1] = one, two
        for t in range(step + 2, tiles):
            total = jnp.where(inside, 0.0, held[t])
            for j, column in enumerate(columns(held[t])):
                total = total - column * line[j]
            held[t] = total
        plain.append(jnp.where(before, rows, 0.0))
        rows = line[0]
        for j in range(1, PIVOTS):
            rows = jnp.where(sub == j, line[j], rows)
        scaled_rows.append(jnp.where(before, rows, 0.0))
        for piece in pieces[step * len(pieces) // tiles : (step + 1) * len(pieces) // tiles]:
            piece()
    high, low = split(jnp.concatenate(plain, axis=0))
    left = jnp.concatenate([high, low, high, low], axis=0)
    high, low = split(jnp.concatenate(scaled_rows, axis=0))
    right = jnp.concatenate([high, high, low, low], axis=0)
    return lax.dot_general(
        left, right, (((0,), (0,)), ((), ())), preferred_element_type=jnp.float32
    )


def factor_kernel(feat, upper, lower, work, inv_ref, sketch, right, wide, left, sem):
    size = work.shape[0]
    blocks = size // BLOCK
    feat_count = upper.shape[1]
    width = size // feat_count
    copies = []
    for group, pieces in enumerate((upper, lower)):
        for mask in range(feat_count):
            start = pl.multiple_of((feat[0] ^ mask) * width, width)
            copies.append(
                pltpu.make_async_copy(
                    pieces.at[:, mask],
                    sketch.at[group, :, :, pl.ds(start, width)],
                    sem.at[group, mask],
                )
            )
    for copy in copies:
        copy.start()
    for copy in copies:
        copy.wait()
    samples = sketch.shape[0] * sketch.shape[1] * sketch.shape[2]
    chunks = size // CHUNK

    def chunk(c):
        return slice(c * CHUNK, (c + 1) * CHUNK)

    def gram(m, _):
        start = pl.multiple_of(m * CHUNK, CHUNK)
        here = pl.ds(start, CHUNK)
        for c in range(chunks):

            @pl.when(c >= m)
            def _():
                product = lax.dot_general(
                    sketch[:, :, :, here].reshape(samples, CHUNK),
                    sketch[:, :, :, chunk(c)].reshape(samples, CHUNK),
                    (((0,), (0,)), ((), ())),
                    preferred_element_type=jnp.float32,
                )
                row = start + lax.broadcasted_iota(jnp.int32, product.shape, 0)
                col = c * CHUNK + lax.broadcasted_iota(jnp.int32, product.shape, 1)
                work[here, chunk(c)] = jnp.where(row == col, product + REG / D, product)

        return 0

    lax.fori_loop(0, chunks, gram, 0)

    def stage(k, c, lowest):
        here = pl.ds(pl.multiple_of(k * BLOCK, BLOCK), BLOCK)
        panel = work[here, chunk(c)]
        if lowest <= c <= lowest + GROUP * BLOCK // CHUNK:
            row = lax.broadcasted_iota(jnp.int32, panel.shape, 0)
            col = c * CHUNK - k * BLOCK + lax.broadcasted_iota(jnp.int32, panel.shape, 1)
            unit = jnp.where(row == col, 1.0, 0.0)
            panel = jnp.where((col >= 0) & (col < BLOCK), unit, panel)
            work[here, chunk(c)] = panel
        high, low = split(panel)
        right[0:BLOCK, chunk(c)] = high
        right[BLOCK : 2 * BLOCK, chunk(c)] = high
        right[2 * BLOCK : 3 * BLOCK, chunk(c)] = low
        right[3 * BLOCK : 4 * BLOCK, chunk(c)] = low
        if c >= lowest:
            high, low = split(panel.T)
            wide[chunk(c), :] = jnp.concatenate([high, low, high, low], axis=1)

    def finish(k, inverse, lowest):
        inv_ref[pl.ds(pl.multiple_of(k * BLOCK, BLOCK), BLOCK), :] = inverse
        high, low = split(inverse)
        diag = jnp.concatenate([high, high, low, low], axis=0)
        for c in range(lowest, chunks):
            scaled = jnp.dot(wide[chunk(c), :], diag, preferred_element_type=jnp.float32)
            place = c * CHUNK + lax.broadcasted_iota(jnp.int32, (CHUNK, BLOCK), 0)
            high, low = split(jnp.where(place >= (k + 1) * BLOCK, scaled, 0.0))
            left[chunk(c), :] = jnp.concatenate([high, low, high, low], axis=1)

    def update(k, m, c, lowest):
        product = jnp.dot(
            left[chunk(m), :], right[:, chunk(c)], preferred_element_type=jnp.float32
        )
        value = work[chunk(m), chunk(c)]
        if lowest <= c < lowest + GROUP * BLOCK // CHUNK:
            row = m * CHUNK + lax.broadcasted_iota(jnp.int32, value.shape, 0)
            col = c * CHUNK + lax.broadcasted_iota(jnp.int32, value.shape, 1)
            fresh = (col >= k * BLOCK) & (col < (k + 1) * BLOCK) & (row >= (k + 1) * BLOCK)
            value = jnp.where(fresh, 0.0, value)
        work[chunk(m), chunk(c)] = value - product

    inverse = invert_block(work[0:BLOCK, 0:BLOCK])
    for c in range(chunks):
        stage(0, c, 0)
    finish(0, inverse, 0)
    for first in range(0, blocks, GROUP):
        lowest = first * BLOCK // CHUNK
        settled = lowest + GROUP * BLOCK // CHUNK

        def outer(k, _):
            following = pl.ds(pl.multiple_of((k + 1) * BLOCK, BLOCK), BLOCK)
            block = work[following, following] - jnp.dot(
                left[following, :], right[:, following], preferred_element_type=jnp.float32
            )
            pieces = []
            for c in range(chunks):
                for m in range(lowest, chunks):
                    if c < settled or c >= m:
                        pieces.append(functools.partial(update, k, m, c, lowest))
                pieces.append(functools.partial(stage, k + 1, c, lowest))
            finish(k + 1, invert_block(block, pieces), lowest)
            return 0

        lax.fori_loop(first, min(first + GROUP, blocks - 1), outer, 0)
    for k in range(blocks):
        last = k // GROUP * GROUP + GROUP
        if k + 1 < last:
            work[k * BLOCK : (k + 1) * BLOCK, (k + 1) * BLOCK : last * BLOCK] = jnp.zeros(
                (BLOCK, (last - k - 1) * BLOCK), jnp.float32
            )


VMEM = pl.BlockSpec(memory_space=pltpu.VMEM)


def factor(feat, upper, lower, interpret=False):
    ex_count, feat_count, rows, width = upper.shape
    size = feat_count * width
    return pl.pallas_call(
        factor_kernel,
        in_specs=[
            pl.BlockSpec(memory_space=pltpu.SMEM),
            pl.BlockSpec(memory_space=pl.ANY),
            pl.BlockSpec(memory_space=pl.ANY),
        ],
        out_specs=[VMEM, VMEM],
        out_shape=[
            pltpu.VMEM((size, size), jnp.float32),
            pltpu.VMEM((size, BLOCK), jnp.float32),
        ],
        scratch_shapes=[
            pltpu.VMEM((2, ex_count, rows, size), jnp.bfloat16),
            pltpu.VMEM((4 * BLOCK, size), jnp.bfloat16),
            pltpu.VMEM((size, 4 * BLOCK), jnp.bfloat16),
            pltpu.VMEM((size, 4 * BLOCK), jnp.bfloat16),
            pltpu.SemaphoreType.DMA((2, feat_count)),
        ],
        compiler_params=pltpu.CompilerParams(vmem_limit_bytes=36 * 2**20),
        interpret=interpret,
    )(feat, upper, lower)


def apply_inverse(lower, inverses, residual, column):
    size = residual.shape[1]
    blocks = size // BLOCK
    eye = lax.broadcasted_iota(jnp.int32, (BLOCK, BLOCK), 0) == lax.broadcasted_iota(
        jnp.int32, (BLOCK, BLOCK), 1
    )
    for group in range(0, blocks, GROUP):
        used = group + GROUP

        def down(k, _):
            here = pl.ds(pl.multiple_of(k * BLOCK, BLOCK), BLOCK)
            sums = jnp.zeros((BLOCK, BLOCK), jnp.float32)
            for c in range(used):
                cols = slice(c * BLOCK, (c + 1) * BLOCK)
                sums = sums + lower[here, cols] * residual[:, cols]
            middle = jnp.sum(sums, axis=1, keepdims=True)
            row = jnp.sum(inverses[here, :] * middle, axis=0, keepdims=True)
            middle = jnp.sum(jnp.where(eye, row, 0.0), axis=1, keepdims=True)
            column[here, :] = jnp.broadcast_to(middle, (BLOCK, BLOCK))
            return 0

        lax.fori_loop(group, used, down, 0, unroll=True)
    total = tuple(jnp.zeros((8, BLOCK), jnp.float32) for _ in range(blocks))
    for group in range(0, blocks, GROUP):
        used = group + GROUP

        def up(t, total):
            here = pl.ds(pl.multiple_of(t * 32, 32), 32)
            middle = column[here, :]
            fresh = list(total)
            for c in range(used):
                cols = slice(c * BLOCK, (c + 1) * BLOCK)
                product = lower[here, cols] * middle
                fresh[c] = fresh[c] + jnp.sum(product.reshape(4, 8, BLOCK), axis=0)
            return tuple(fresh)

        total = lax.fori_loop(group * BLOCK // 32, used * BLOCK // 32, up, total)
    return jnp.concatenate([jnp.sum(t, axis=0, keepdims=True) for t in total], axis=1)


def curve(rows_ref, direction):
    count, size = rows_ref.shape
    blocks = size // BLOCK
    high = 16

    def step(i, total):
        here = pl.ds(pl.multiple_of(i * high, high), high)
        tile = rows_ref[here, :].astype(jnp.float32)
        sums = jnp.zeros((high, BLOCK), jnp.float32)
        for c in range(blocks):
            cols = slice(c * BLOCK, (c + 1) * BLOCK)
            sums = sums + tile[:, cols] * direction[:, cols]
        column = jnp.sum(sums, axis=1, keepdims=True)
        fresh = list(total)
        for c in range(blocks):
            product = tile[:, c * BLOCK : (c + 1) * BLOCK] * column
            fresh[c] = fresh[c] + (product[:8] + product[8:])
        return tuple(fresh)

    total = tuple(jnp.zeros((8, BLOCK), jnp.float32) for _ in range(blocks))
    total = lax.fori_loop(0, count // high, step, total, unroll=4)
    return jnp.concatenate([jnp.sum(t, axis=0, keepdims=True) for t in total], axis=1)


def dot(left, right):
    return jnp.sum(left * right, axis=1, keepdims=True)


def first_kernel(lower, inverses, rows, residual, direction, inner, curved, column):
    solved = apply_inverse(lower, inverses, residual[...], column)
    inner[...] = dot(residual[...], solved)
    direction[...] = solved
    curved[...] = curve(rows, direction)


def next_kernel(
    total_rows, lower, inverses, rows, sums, solution, residual, direction, inner,
    solution_out, residual_out, direction_out, inner_out, curved_out, column,
):
    ahead = direction[...]
    curved = sums[...] / total_rows + (REG / D) * ahead
    size = inner[...] / dot(ahead, curved)
    solution_out[...] = solution[...] + size * ahead
    left = residual[...] - size * curved
    residual_out[...] = left
    solved = apply_inverse(lower, inverses, left, column)
    fresh = dot(left, solved)
    inner_out[...] = fresh
    direction_out[...] = solved + fresh / inner[...] * ahead
    curved_out[...] = curve(rows, direction_out)


def last_kernel(total_rows, sums, solution, direction, inner, radius, out):
    ahead = direction[...]
    curved = sums[...] / total_rows + (REG / D) * ahead
    size = inner[...] / dot(ahead, curved)
    full = solution[...] + size * ahead
    length_sq = dot(full, full)
    scale = jnp.minimum(1.0, radius[...] * math.sqrt(D) / jnp.sqrt(length_sq + 1e-06))
    out[...] = scale * full


def call(kernel, shapes, args, scratch=()):
    args = list(args)
    for place, value in enumerate(args):
        if value.size >= BLOCK * D:
            args[place] = pltpu.with_memory_space_constraint(value, pltpu.VMEM)
    return pl.pallas_call(
        kernel,
        in_specs=[VMEM] * len(args),
        out_specs=[VMEM] * len(shapes),
        out_shape=[jax.ShapeDtypeStruct(shape, jnp.float32) for shape in shapes],
        scratch_shapes=scratch,
        compiler_params=pltpu.CompilerParams(vmem_limit_bytes=8 * 2**20),
    )(*args)


def exchange(value, axis):
    count = lax.axis_size(axis)
    pieces = [value]
    for mask in range(1, count):
        pieces.append(lax.ppermute(value, axis, [(s, s ^ mask) for s in range(count)]))
    return pieces


def swap(value, axis, bit):
    mask = 2**bit
    return lax.ppermute(value, axis, [(s, s ^ mask) for s in range(lax.axis_size(axis))])


def bit_places(order):
    places = [0]
    for bit in reversed(order):
        places = places + [place | 2**bit for place in places]
    return places


def sampled_mix(samples, places, signed):
    count = lax.axis_size("ex")
    grid = samples.reshape(count * 2, -1)
    upward = list(range(1, count.bit_length() - 1))
    downward = upward[::-1]
    wanted = [(q, 0) for q in bit_places(upward)] + [(q, 1) for q in bit_places(downward)]
    numbers = jnp.array([[q ^ 1, half] for q, half in wanted] + [[q, half] for q, half in wanted])
    rows = grid[(numbers[:, 0] ^ lax.axis_index("ex")) * 2 + numbers[:, 1]].reshape(2, -1)

    def mix(chosen):
        odd = lax.population_count(chosen[:, None] & places[None, :]) & 1
        table = (1 - 2 * odd).astype(jnp.bfloat16)
        return jnp.dot(table, signed, preferred_element_type=jnp.float32)

    total = swap(mix(rows[0]).astype(jnp.float16), "ex", 0).astype(jnp.float32) + mix(rows[1])
    parts = list(jnp.split(total, 2))
    for bits in zip(upward, downward):
        halves = [jnp.split(part, 2) for part in parts]
        got = [
            swap(half[1].astype(jnp.float16), "ex", bit) for half, bit in zip(halves, bits)
        ]
        got = lax.optimization_barrier(got)
        parts = [half[0] + other.astype(jnp.float32) for half, other in zip(halves, got)]
    return parts


def butterfly(value):
    for axis in ("ex", "feat"):
        count = lax.axis_size(axis)
        mask = 1
        while mask < count:
            value = value + lax.ppermute(value, axis, [(s, s ^ mask) for s in range(count)])
            mask = mask * 2
    return value


def local(features, weights, labels, signs, samples, radius):
    highest = lax.Precision.HIGHEST
    row_count, feat_width = features.shape
    ex_count = lax.axis_size("ex")
    ex_index = lax.axis_index("ex")
    feat_count = lax.axis_size("feat")
    feat_index = lax.axis_index("feat")
    total_rows = row_count * ex_count
    sample_count = samples.shape[0]
    dense = features.astype(jnp.float32)
    margins = sum(exchange(jnp.dot(dense, weights, precision=highest), "feat"))
    probability = 1.0 / (1.0 + jnp.exp(-margins))
    curvature = probability * (1.0 - probability)
    weighted = (jnp.sqrt(curvature)[:, None] * dense).astype(jnp.bfloat16)
    signed = weighted * signs.astype(jnp.bfloat16)[:, None]
    places = ex_index * row_count + lax.iota(jnp.int32, row_count)
    scale = 1.0 / math.sqrt(total_rows * sample_count)
    upper, lower = [
        (part * scale).astype(jnp.bfloat16) for part in sampled_mix(samples, places, signed)
    ]
    upper = jnp.stack(exchange(upper, "feat"))
    upper, lower = lax.optimization_barrier((upper, lower))
    lower = jnp.stack(exchange(lower, "feat"))
    upper, lower = [lax.all_gather(value, "ex", axis=0) for value in (upper, lower)]
    lower, inverses = factor(feat_index.astype(jnp.int32)[None], upper, lower)

    grad_part = jnp.dot(probability - labels.astype(jnp.float32), dense, precision=highest)
    own_weights = jnp.where(ex_index == 0, REG / D, 0.0) * weights
    wide = jnp.zeros((feat_count, feat_width), jnp.float32)
    wide = lax.dynamic_update_slice_in_dim(
        wide, (grad_part / total_rows + own_weights)[None], feat_index, 0
    )
    residual = -butterfly(wide.reshape(1, D))
    own_rows = lax.all_to_all(weighted, "feat", split_axis=0, concat_axis=1, tiled=True)

    row, one = (1, D), (1, 1)
    scratch = [pltpu.VMEM((D, BLOCK), jnp.float32)]
    direction, inner, curved = call(
        first_kernel, [row, one, row], [lower, inverses, own_rows, residual], scratch
    )
    solution = jnp.zeros(row, jnp.float32)
    following = functools.partial(next_kernel, total_rows)
    for _ in range(ITERS - 1):
        solution, residual, direction, inner, curved = call(
            following,
            [row, row, row, one, row],
            [lower, inverses, own_rows, butterfly(curved), solution, residual, direction, inner],
            scratch,
        )
    (step,) = call(
        functools.partial(last_kernel, total_rows),
        [row],
        [butterfly(curved), solution, direction, inner, radius[None, :]],
    )
    own = lax.dynamic_slice_in_dim(step[0], feat_index * feat_width, feat_width, 0)
    return weights + own


def solution(mesh):
    in_specs = (P("ex", "feat"), P("feat"), P("ex"), P("ex"), P(), P())
    out_specs = P("feat")
    return jax.shard_map(local, mesh=mesh, in_specs=in_specs, out_specs=out_specs, check_vma=False)
```

```python
import functools
import math

import jax
import jax.numpy as jnp
from jax import lax
from jax.experimental import pallas as pl
from jax.experimental.pallas import tpu as pltpu
from jax.sharding import PartitionSpec as P

D = 2048
ITERS = 4
REG = 0.02
BLOCK = 128
PIVOTS = 8
CHUNK = 256
GROUP = 4


def split(value):
    high = value.astype(jnp.bfloat16)
    low = (value - high.astype(jnp.float32)).astype(jnp.bfloat16)
    return high, low


def invert_block(block, pieces=()):
    tiles = BLOCK // PIVOTS
    slots = BLOCK // 2
    lane = lax.broadcasted_iota(jnp.int32, (PIVOTS, BLOCK), 1)
    sub = lax.broadcasted_iota(jnp.int32, (PIVOTS, BLOCK), 0)
    shape = (PIVOTS, BLOCK)
    held = [block[t * PIVOTS : (t + 1) * PIVOTS, :] for t in range(tiles)]
    plain, scaled_rows = [], []
    for step in range(tiles):
        first = step * PIVOTS
        rows = held[step]
        inside = (lane >= first) & (lane < first + PIVOTS)
        before = lane < first + PIVOTS
        last = step + 1 == tiles

        def columns(tile):
            return [
                jnp.broadcast_to(tile[:, first + j : first + j + 1], shape) for j in range(PIVOTS)
            ]

        wide = columns(rows)
        cell = {}
        for j in range(PIVOTS):
            for i in range(j, PIVOTS):
                cell[i, j] = jnp.broadcast_to(wide[j][i : i + 1, :], shape)
        rows = jnp.where(inside, (lane - first == sub).astype(jnp.float32), rows)
        line = [jnp.broadcast_to(rows[i : i + 1, :], shape) for i in range(PIVOTS)]
        if not last:
            ahead = columns(held[step + 1])
            total = jnp.where(inside, 0.0, held[step + 1])
        scaled = {}
        pairs = []
        for j in range(0, PIVOTS, 2):
            a, b, d = cell[j, j], cell[j + 1, j], cell[j + 1, j + 1]
            inverse = 1.0 / (a * d - b * b)
            slot = (step * PIVOTS + j) // 2
            for piece in pieces[slot * len(pieces) // slots : (slot + 1) * len(pieces) // slots]:
                piece()
            pairs.append((a * inverse, b * inverse, d * inverse))
            for i in range(j + 2, PIVOTS):
                one, two = cell[i, j], cell[i, j + 1]
                scaled[i, j] = one * d - two * b
                scaled[i, j + 1] = two * a - one * b
            for i in range(j + 2, PIVOTS):
                for m in range(j + 2, i + 1):
                    product = scaled[i, j] * cell[m, j] + scaled[i, j + 1] * cell[m, j + 1]
                    cell[i, m] = cell[i, m] - product * inverse
            if not last:
                one = ahead[j] * d - ahead[j + 1] * b
                two = ahead[j + 1] * a - ahead[j] * b
                for m in range(j + 2, PIVOTS):
                    product = one * cell[m, j] + two * cell[m, j + 1]
                    ahead[m] = ahead[m] - product * inverse
                total = total - (one * line[j] + two * line[j + 1]) * inverse
            for i in range(j + 2, PIVOTS):
                scaled[i, j] = scaled[i, j] * inverse
                scaled[i, j + 1] = scaled[i, j + 1] * inverse
                line[i] = line[i] - (scaled[i, j] * line[j] + scaled[i, j + 1] * line[j + 1])
        if not last:
            held[step + 1] = total
        for j in range(PIVOTS - 2, -1, -2):
            a, b, d = pairs[j // 2]
            one = line[j] * d - line[j + 1] * b
            two = line[j + 1] * a - line[j] * b
            for i in range(j + 2, PIVOTS):
                one = one - scaled[i, j] * line[i]
                two = two - scaled[i, j + 1] * line[i]
            line[j], line[j + 1] = one, two
        for t in range(step + 2, tiles):
            total = jnp.where(inside, 0.0, held[t])
            for j, column in enumerate(columns(held[t])):
                total = total - column * line[j]
            held[t] = total
        plain.append(jnp.where(before, rows, 0.0))
        rows = line[0]
        for j in range(1, PIVOTS):
            rows = jnp.where(sub == j, line[j], rows)
        scaled_rows.append(jnp.where(before, rows, 0.0))
    high, low = split(jnp.concatenate(plain, axis=0))
    left = jnp.concatenate([high, low, high, low], axis=0)
    high, low = split(jnp.concatenate(scaled_rows, axis=0))
    right = jnp.concatenate([high, high, low, low], axis=0)
    return lax.dot_general(
        left, right, (((0,), (0,)), ((), ())), preferred_element_type=jnp.float32
    )


def factor_kernel(feat, pieces, work, inv_ref, sketch, right, wide, left, sem):
    size = work.shape[0]
    blocks = size // BLOCK
    feat_count = pieces.shape[1]
    width = size // feat_count
    copies = []
    for mask in range(feat_count):
        start = pl.multiple_of((feat[0] ^ mask) * width, width)
        copies.append(
            pltpu.make_async_copy(
                pieces.at[:, mask], sketch.at[:, :, pl.ds(start, width)], sem.at[mask]
            )
        )
    for copy in copies:
        copy.start()
    for copy in copies:
        copy.wait()
    samples = sketch.shape[0] * sketch.shape[1]
    chunks = size // CHUNK

    def chunk(c):
        return slice(c * CHUNK, (c + 1) * CHUNK)

    def gram(m, _):
        start = pl.multiple_of(m * CHUNK, CHUNK)
        here = pl.ds(start, CHUNK)
        for c in range(chunks):

            @pl.when(c >= m)
            def _():
                product = lax.dot_general(
                    sketch[:, :, here].reshape(samples, CHUNK),
                    sketch[:, :, chunk(c)].reshape(samples, CHUNK),
                    (((0,), (0,)), ((), ())),
                    preferred_element_type=jnp.float32,
                )
                row = start + lax.broadcasted_iota(jnp.int32, product.shape, 0)
                col = c * CHUNK + lax.broadcasted_iota(jnp.int32, product.shape, 1)
                work[here, chunk(c)] = jnp.where(row == col, product + REG / D, product)

        return 0

    lax.fori_loop(0, chunks, gram, 0)

    def stage(k, c, lowest):
        here = pl.ds(pl.multiple_of(k * BLOCK, BLOCK), BLOCK)
        panel = work[here, chunk(c)]
        if lowest <= c <= lowest + GROUP * BLOCK // CHUNK:
            row = lax.broadcasted_iota(jnp.int32, panel.shape, 0)
            col = c * CHUNK - k * BLOCK + lax.broadcasted_iota(jnp.int32, panel.shape, 1)
            unit = jnp.where(row == col, 1.0, 0.0)
            panel = jnp.where((col >= 0) & (col < BLOCK), unit, panel)
            work[here, chunk(c)] = panel
        high, low = split(panel)
        right[0:BLOCK, chunk(c)] = high
        right[BLOCK : 2 * BLOCK, chunk(c)] = high
        right[2 * BLOCK : 3 * BLOCK, chunk(c)] = low
        right[3 * BLOCK : 4 * BLOCK, chunk(c)] = low
        if c >= lowest:
            high, low = split(panel.T)
            wide[chunk(c), :] = jnp.concatenate([high, low, high, low], axis=1)

    def finish(k, inverse, lowest):
        inv_ref[pl.ds(pl.multiple_of(k * BLOCK, BLOCK), BLOCK), :] = inverse
        high, low = split(inverse)
        diag = jnp.concatenate([high, high, low, low], axis=0)
        for c in range(lowest, chunks):
            scaled = jnp.dot(wide[chunk(c), :], diag, preferred_element_type=jnp.float32)
            place = c * CHUNK + lax.broadcasted_iota(jnp.int32, (CHUNK, BLOCK), 0)
            high, low = split(jnp.where(place >= (k + 1) * BLOCK, scaled, 0.0))
            left[chunk(c), :] = jnp.concatenate([high, low, high, low], axis=1)

    def update(k, m, c, lowest):
        product = jnp.dot(
            left[chunk(m), :], right[:, chunk(c)], preferred_element_type=jnp.float32
        )
        value = work[chunk(m), chunk(c)]
        if lowest <= c < lowest + GROUP * BLOCK // CHUNK:
            row = m * CHUNK + lax.broadcasted_iota(jnp.int32, value.shape, 0)
            col = c * CHUNK + lax.broadcasted_iota(jnp.int32, value.shape, 1)
            fresh = (col >= k * BLOCK) & (col < (k + 1) * BLOCK) & (row >= (k + 1) * BLOCK)
            value = jnp.where(fresh, 0.0, value)
        work[chunk(m), chunk(c)] = value - product

    inverse = invert_block(work[0:BLOCK, 0:BLOCK])
    for c in range(chunks):
        stage(0, c, 0)
    finish(0, inverse, 0)
    for first in range(0, blocks, GROUP):
        lowest = first * BLOCK // CHUNK
        settled = lowest + GROUP * BLOCK // CHUNK

        def outer(k, _):
            following = pl.ds(pl.multiple_of((k + 1) * BLOCK, BLOCK), BLOCK)
            block = work[following, following] - jnp.dot(
                left[following, :], right[:, following], preferred_element_type=jnp.float32
            )
            pieces = []
            for c in range(chunks):
                for m in range(lowest, chunks):
                    if c < settled or c >= m:
                        pieces.append(functools.partial(update, k, m, c, lowest))
                pieces.append(functools.partial(stage, k + 1, c, lowest))
            finish(k + 1, invert_block(block, pieces), lowest)
            return 0

        lax.fori_loop(first, min(first + GROUP, blocks - 1), outer, 0)
    for k in range(blocks):
        last = k // GROUP * GROUP + GROUP
        if k + 1 < last:
            work[k * BLOCK : (k + 1) * BLOCK, (k + 1) * BLOCK : last * BLOCK] = jnp.zeros(
                (BLOCK, (last - k - 1) * BLOCK), jnp.float32
            )


VMEM = pl.BlockSpec(memory_space=pltpu.VMEM)


def factor(feat, pieces, interpret=False):
    ex_count, feat_count, rows, width = pieces.shape
    size = feat_count * width
    return pl.pallas_call(
        factor_kernel,
        in_specs=[
            pl.BlockSpec(memory_space=pltpu.SMEM),
            pl.BlockSpec(memory_space=pl.ANY),
        ],
        out_specs=[VMEM, VMEM],
        out_shape=[
            pltpu.VMEM((size, size), jnp.float32),
            pltpu.VMEM((size, BLOCK), jnp.float32),
        ],
        scratch_shapes=[
            pltpu.VMEM((ex_count, rows, size), jnp.bfloat16),
            pltpu.VMEM((4 * BLOCK, size), jnp.bfloat16),
            pltpu.VMEM((size, 4 * BLOCK), jnp.bfloat16),
            pltpu.VMEM((size, 4 * BLOCK), jnp.bfloat16),
            pltpu.SemaphoreType.DMA((feat_count,)),
        ],
        compiler_params=pltpu.CompilerParams(vmem_limit_bytes=36 * 2**20),
        interpret=interpret,
    )(feat, pieces)


def apply_inverse(lower, inverses, residual, column):
    size = residual.shape[1]
    blocks = size // BLOCK
    eye = lax.broadcasted_iota(jnp.int32, (BLOCK, BLOCK), 0) == lax.broadcasted_iota(
        jnp.int32, (BLOCK, BLOCK), 1
    )
    for group in range(0, blocks, GROUP):
        used = group + GROUP

        def down(k, _):
            here = pl.ds(pl.multiple_of(k * BLOCK, BLOCK), BLOCK)
            sums = jnp.zeros((BLOCK, BLOCK), jnp.float32)
            for c in range(used):
                cols = slice(c * BLOCK, (c + 1) * BLOCK)
                sums = sums + lower[here, cols] * residual[:, cols]
            middle = jnp.sum(sums, axis=1, keepdims=True)
            row = jnp.sum(inverses[here, :] * middle, axis=0, keepdims=True)
            middle = jnp.sum(jnp.where(eye, row, 0.0), axis=1, keepdims=True)
            column[here, :] = jnp.broadcast_to(middle, (BLOCK, BLOCK))
            return 0

        lax.fori_loop(group, used, down, 0, unroll=True)
    total = tuple(jnp.zeros((8, BLOCK), jnp.float32) for _ in range(blocks))
    for group in range(0, blocks, GROUP):
        used = group + GROUP

        def up(t, total):
            here = pl.ds(pl.multiple_of(t * 32, 32), 32)
            middle = column[here, :]
            fresh = list(total)
            for c in range(used):
                cols = slice(c * BLOCK, (c + 1) * BLOCK)
                product = lower[here, cols] * middle
                fresh[c] = fresh[c] + jnp.sum(product.reshape(4, 8, BLOCK), axis=0)
            return tuple(fresh)

        total = lax.fori_loop(group * BLOCK // 32, used * BLOCK // 32, up, total)
    return jnp.concatenate([jnp.sum(t, axis=0, keepdims=True) for t in total], axis=1)


def curve(rows_ref, direction):
    count, size = rows_ref.shape
    blocks = size // BLOCK
    high = 16

    def step(i, total):
        here = pl.ds(pl.multiple_of(i * high, high), high)
        tile = rows_ref[here, :].astype(jnp.float32)
        sums = jnp.zeros((high, BLOCK), jnp.float32)
        for c in range(blocks):
            cols = slice(c * BLOCK, (c + 1) * BLOCK)
            sums = sums + tile[:, cols] * direction[:, cols]
        column = jnp.sum(sums, axis=1, keepdims=True)
        fresh = list(total)
        for c in range(blocks):
            product = tile[:, c * BLOCK : (c + 1) * BLOCK] * column
            fresh[c] = fresh[c] + (product[:8] + product[8:])
        return tuple(fresh)

    total = tuple(jnp.zeros((8, BLOCK), jnp.float32) for _ in range(blocks))
    total = lax.fori_loop(0, count // high, step, total, unroll=4)
    return jnp.concatenate([jnp.sum(t, axis=0, keepdims=True) for t in total], axis=1)


def dot(left, right):
    return jnp.sum(left * right, axis=1, keepdims=True)


def first_kernel(lower, inverses, rows, residual, direction, inner, curved, column):
    solved = apply_inverse(lower, inverses, residual[...], column)
    inner[...] = dot(residual[...], solved)
    direction[...] = solved
    curved[...] = curve(rows, direction)


def next_kernel(
    total_rows, lower, inverses, rows, sums, solution, residual, direction, inner,
    solution_out, residual_out, direction_out, inner_out, curved_out, column,
):
    ahead = direction[...]
    curved = sums[...] / total_rows + (REG / D) * ahead
    size = inner[...] / dot(ahead, curved)
    solution_out[...] = solution[...] + size * ahead
    left = residual[...] - size * curved
    residual_out[...] = left
    solved = apply_inverse(lower, inverses, left, column)
    fresh = dot(left, solved)
    inner_out[...] = fresh
    direction_out[...] = solved + fresh / inner[...] * ahead
    curved_out[...] = curve(rows, direction_out)


def last_kernel(total_rows, sums, solution, direction, inner, radius, out):
    ahead = direction[...]
    curved = sums[...] / total_rows + (REG / D) * ahead
    size = inner[...] / dot(ahead, curved)
    full = solution[...] + size * ahead
    length_sq = dot(full, full)
    scale = jnp.minimum(1.0, radius[...] * math.sqrt(D) / jnp.sqrt(length_sq + 1e-06))
    out[...] = scale * full


def call(kernel, shapes, args, scratch=()):
    args = list(args)
    for place, value in enumerate(args):
        if value.size >= BLOCK * D:
            args[place] = pltpu.with_memory_space_constraint(value, pltpu.VMEM)
    return pl.pallas_call(
        kernel,
        in_specs=[VMEM] * len(args),
        out_specs=[VMEM] * len(shapes),
        out_shape=[jax.ShapeDtypeStruct(shape, jnp.float32) for shape in shapes],
        scratch_shapes=scratch,
        compiler_params=pltpu.CompilerParams(vmem_limit_bytes=8 * 2**20),
    )(*args)


def exchange(value, axis):
    count = lax.axis_size(axis)
    pieces = [value]
    for mask in range(1, count):
        pieces.append(lax.ppermute(value, axis, [(s, s ^ mask) for s in range(count)]))
    return pieces


def swap(value, axis, bit):
    mask = 2**bit
    return lax.ppermute(value, axis, [(s, s ^ mask) for s in range(lax.axis_size(axis))])


def bit_places(order):
    places = [0]
    for bit in reversed(order):
        places = places + [place | 2**bit for place in places]
    return places


def sampled_mix(samples, places, signed):
    count = lax.axis_size("ex")
    grid = samples.reshape(count * 2, -1)
    upward = list(range(1, count.bit_length() - 1))
    downward = upward[::-1]
    wanted = [(q, 0) for q in bit_places(upward)] + [(q, 1) for q in bit_places(downward)]
    numbers = jnp.array([[q ^ 1, half] for q, half in wanted] + [[q, half] for q, half in wanted])
    rows = grid[(numbers[:, 0] ^ lax.axis_index("ex")) * 2 + numbers[:, 1]].reshape(2, -1)

    def mix(chosen):
        odd = lax.population_count(chosen[:, None] & places[None, :]) & 1
        table = (1 - 2 * odd).astype(jnp.bfloat16)
        return jnp.dot(table, signed, preferred_element_type=jnp.float32)

    total = swap(mix(rows[0]).astype(jnp.float16), "ex", 0).astype(jnp.float32) + mix(rows[1])
    parts = list(jnp.split(total, 2))
    for bits in zip(upward, downward):
        halves = [jnp.split(part, 2) for part in parts]
        got = [
            swap(half[1].astype(jnp.float16), "ex", bit) for half, bit in zip(halves, bits)
        ]
        got = lax.optimization_barrier(got)
        parts = [half[0] + other.astype(jnp.float32) for half, other in zip(halves, got)]
    return parts


def butterfly(value, axes=("ex", "feat")):
    for axis in axes:
        count = lax.axis_size(axis)
        for bit in range(count.bit_length() - 1):
            value = value + swap(value, axis, bit)
    return value


def local(features, weights, labels, signs, samples, radius):
    highest = lax.Precision.HIGHEST
    row_count, feat_width = features.shape
    ex_count = lax.axis_size("ex")
    ex_index = lax.axis_index("ex")
    feat_count = lax.axis_size("feat")
    feat_index = lax.axis_index("feat")
    total_rows = row_count * ex_count
    sample_count = samples.shape[0]
    dense = features.astype(jnp.float32)
    margins = butterfly(jnp.dot(dense, weights, precision=highest), ("feat",))
    probability = 1.0 / (1.0 + jnp.exp(-margins))
    curvature = probability * (1.0 - probability)
    weighted = (jnp.sqrt(curvature)[:, None] * dense).astype(jnp.bfloat16)
    signed = weighted * signs.astype(jnp.bfloat16)[:, None]
    places = ex_index * row_count + lax.iota(jnp.int32, row_count)
    scale = 1.0 / math.sqrt(total_rows * sample_count)
    sketch = (jnp.concatenate(sampled_mix(samples, places, signed)) * scale).astype(jnp.bfloat16)
    wide_sketch = jnp.stack(exchange(sketch, "feat"))
    pieces = lax.all_gather(wide_sketch, "ex", axis=0)
    lower, inverses = factor(feat_index.astype(jnp.int32)[None], pieces)

    grad_part = jnp.dot(probability - labels.astype(jnp.float32), dense, precision=highest)
    own_weights = jnp.where(ex_index == 0, REG / D, 0.0) * weights
    wide = jnp.zeros((feat_count, feat_width), jnp.float32)
    wide = lax.dynamic_update_slice_in_dim(
        wide, (grad_part / total_rows + own_weights)[None], feat_index, 0
    )
    residual = -butterfly(wide.reshape(1, D))
    own_rows = lax.all_to_all(weighted, "feat", split_axis=0, concat_axis=1, tiled=True)

    row, one = (1, D), (1, 1)
    scratch = [pltpu.VMEM((D, BLOCK), jnp.float32)]
    direction, inner, curved = call(
        first_kernel, [row, one, row], [lower, inverses, own_rows, residual], scratch
    )
    solution = jnp.zeros(row, jnp.float32)
    following = functools.partial(next_kernel, total_rows)
    for _ in range(ITERS - 1):
        solution, residual, direction, inner, curved = call(
            following,
            [row, row, row, one, row],
            [lower, inverses, own_rows, butterfly(curved), solution, residual, direction, inner],
            scratch,
        )
    (step,) = call(
        functools.partial(last_kernel, total_rows),
        [row],
        [butterfly(curved), solution, direction, inner, radius[None, :]],
    )
    own = lax.dynamic_slice_in_dim(step[0], feat_index * feat_width, feat_width, 0)
    return weights + own


def solution(mesh):
    in_specs = (P("ex", "feat"), P("feat"), P("ex"), P("ex"), P(), P())
    out_specs = P("feat")
    return jax.shard_map(local, mesh=mesh, in_specs=in_specs, out_specs=out_specs, check_vma=False)
```

```python
import functools
import math

import jax
import jax.numpy as jnp
from jax import lax
from jax.experimental import pallas as pl
from jax.experimental.pallas import tpu as pltpu
from jax.sharding import PartitionSpec as P

D = 2048
ITERS = 4
REG = 0.02
BLOCK = 128
PIVOTS = 8
CHUNK = 256
GROUP = 4


def split(value):
    high = value.astype(jnp.bfloat16)
    low = (value - high.astype(jnp.float32)).astype(jnp.bfloat16)
    return high, low


def invert_block(block, pieces=()):
    tiles = BLOCK // PIVOTS
    slots = BLOCK // 2
    lane = lax.broadcasted_iota(jnp.int32, (PIVOTS, BLOCK), 1)
    sub = lax.broadcasted_iota(jnp.int32, (PIVOTS, BLOCK), 0)
    shape = (PIVOTS, BLOCK)
    held = [block[t * PIVOTS : (t + 1) * PIVOTS, :] for t in range(tiles)]
    plain, scaled_rows = [], []
    for step in range(tiles):
        first = step * PIVOTS
        rows = held[step]
        inside = (lane >= first) & (lane < first + PIVOTS)
        before = lane < first + PIVOTS
        last = step + 1 == tiles

        def columns(tile):
            return [
                jnp.broadcast_to(tile[:, first + j : first + j + 1], shape) for j in range(PIVOTS)
            ]

        wide = columns(rows)
        cell = {}
        for j in range(PIVOTS):
            for i in range(j, PIVOTS):
                cell[i, j] = jnp.broadcast_to(wide[j][i : i + 1, :], shape)
        rows = jnp.where(inside, (lane - first == sub).astype(jnp.float32), rows)
        line = [jnp.broadcast_to(rows[i : i + 1, :], shape) for i in range(PIVOTS)]
        if not last:
            ahead = columns(held[step + 1])
            total = jnp.where(inside, 0.0, held[step + 1])
        scaled = {}
        pairs = []
        for j in range(0, PIVOTS, 2):
            a, b, d = cell[j, j], cell[j + 1, j], cell[j + 1, j + 1]
            inverse = 1.0 / (a * d - b * b)
            slot = (step * PIVOTS + j) // 2
            for piece in pieces[slot * len(pieces) // slots : (slot + 1) * len(pieces) // slots]:
                piece()
            pairs.append((a * inverse, b * inverse, d * inverse))
            for i in range(j + 2, PIVOTS):
                one, two = cell[i, j], cell[i, j + 1]
                scaled[i, j] = one * d - two * b
                scaled[i, j + 1] = two * a - one * b
            for i in range(j + 2, PIVOTS):
                for m in range(j + 2, i + 1):
                    product = scaled[i, j] * cell[m, j] + scaled[i, j + 1] * cell[m, j + 1]
                    cell[i, m] = cell[i, m] - product * inverse
            if not last:
                one = ahead[j] * d - ahead[j + 1] * b
                two = ahead[j + 1] * a - ahead[j] * b
                for m in range(j + 2, PIVOTS):
                    product = one * cell[m, j] + two * cell[m, j + 1]
                    ahead[m] = ahead[m] - product * inverse
                total = total - (one * line[j] + two * line[j + 1]) * inverse
            for i in range(j + 2, PIVOTS):
                scaled[i, j] = scaled[i, j] * inverse
                scaled[i, j + 1] = scaled[i, j + 1] * inverse
                line[i] = line[i] - (scaled[i, j] * line[j] + scaled[i, j + 1] * line[j + 1])
        if not last:
            held[step + 1] = total
        for j in range(PIVOTS - 2, -1, -2):
            a, b, d = pairs[j // 2]
            one = line[j] * d - line[j + 1] * b
            two = line[j + 1] * a - line[j] * b
            for i in range(j + 2, PIVOTS):
                one = one - scaled[i, j] * line[i]
                two = two - scaled[i, j + 1] * line[i]
            line[j], line[j + 1] = one, two
        for t in range(step + 2, tiles):
            total = jnp.where(inside, 0.0, held[t])
            for j, column in enumerate(columns(held[t])):
                total = total - column * line[j]
            held[t] = total
        plain.append(jnp.where(before, rows, 0.0))
        rows = line[0]
        for j in range(1, PIVOTS):
            rows = jnp.where(sub == j, line[j], rows)
        scaled_rows.append(jnp.where(before, rows, 0.0))
    high, low = split(jnp.concatenate(plain, axis=0))
    left = jnp.concatenate([high, low, high, low], axis=0)
    high, low = split(jnp.concatenate(scaled_rows, axis=0))
    right = jnp.concatenate([high, high, low, low], axis=0)
    return lax.dot_general(
        left, right, (((0,), (0,)), ((), ())), preferred_element_type=jnp.float32
    )


def factor_kernel(feat, pieces, work, inv_ref, sketch, turned, right, left, sem):
    size = work.shape[0]
    blocks = size // BLOCK
    feat_count = pieces.shape[1]
    width = size // feat_count
    copies = []
    for mask in range(feat_count):
        start = pl.multiple_of((feat[0] ^ mask) * width, width)
        copies.append(
            pltpu.make_async_copy(
                pieces.at[:, mask], sketch.at[:, :, pl.ds(start, width)], sem.at[mask]
            )
        )
    for copy in copies:
        copy.start()
    for copy in copies:
        copy.wait()
    samples = sketch.shape[0] * sketch.shape[1]
    chunks = size // CHUNK

    def chunk(c):
        return slice(c * CHUNK, (c + 1) * CHUNK)

    def gram(m, _):
        start = pl.multiple_of(m * CHUNK, CHUNK)
        here = pl.ds(start, CHUNK)
        turned[...] = sketch[:, :, here].reshape(samples, CHUNK).T
        for c in range(chunks):

            @pl.when(c >= m)
            def _():
                product = jnp.dot(
                    turned[...],
                    sketch[:, :, chunk(c)].reshape(samples, CHUNK),
                    preferred_element_type=jnp.float32,
                )
                row = start + lax.broadcasted_iota(jnp.int32, product.shape, 0)
                col = c * CHUNK + lax.broadcasted_iota(jnp.int32, product.shape, 1)
                work[here, chunk(c)] = jnp.where(row == col, product + REG / D, product)

        return 0

    lax.fori_loop(0, chunks, gram, 0)

    eye = (
        lax.broadcasted_iota(jnp.int32, (BLOCK, BLOCK), 0)
        == lax.broadcasted_iota(jnp.int32, (BLOCK, BLOCK), 1)
    ).astype(jnp.float32)

    def prepare(k, inverse, lowest):
        here = pl.ds(pl.multiple_of(k * BLOCK, BLOCK), BLOCK)
        inv_ref[here, :] = inverse
        high, low = split(inverse)
        diag = jnp.concatenate([high, high, low, low], axis=0)
        work[here, here] = eye
        for c in range(chunks):
            panel = work[here, chunk(c)]
            high, low = split(panel)
            right[0:BLOCK, chunk(c)] = high
            right[BLOCK : 2 * BLOCK, chunk(c)] = high
            right[2 * BLOCK : 3 * BLOCK, chunk(c)] = low
            right[3 * BLOCK : 4 * BLOCK, chunk(c)] = low
            if c >= lowest:
                high, low = split(panel.T)
                wide = jnp.concatenate([high, low, high, low], axis=1)
                scaled = jnp.dot(wide, diag, preferred_element_type=jnp.float32)
                place = c * CHUNK + lax.broadcasted_iota(jnp.int32, (CHUNK, BLOCK), 0)
                high, low = split(jnp.where(place >= (k + 1) * BLOCK, scaled, 0.0))
                left[chunk(c), :] = jnp.concatenate([high, low, high, low], axis=1)

    def update(k, m, c, lowest):
        product = jnp.dot(
            left[chunk(m), :], right[:, chunk(c)], preferred_element_type=jnp.float32
        )
        value = work[chunk(m), chunk(c)]
        if lowest <= c < lowest + GROUP * BLOCK // CHUNK:
            row = m * CHUNK + lax.broadcasted_iota(jnp.int32, value.shape, 0)
            col = c * CHUNK + lax.broadcasted_iota(jnp.int32, value.shape, 1)
            fresh = (col >= k * BLOCK) & (col < (k + 1) * BLOCK) & (row >= (k + 1) * BLOCK)
            value = jnp.where(fresh, 0.0, value)
        work[chunk(m), chunk(c)] = value - product

    prepare(0, invert_block(work[0:BLOCK, 0:BLOCK]), 0)
    for first in range(0, blocks, GROUP):
        lowest = first * BLOCK // CHUNK
        settled = lowest + GROUP * BLOCK // CHUNK
        wanted = [
            (m, c) for m in range(lowest, chunks) for c in range(chunks) if c < settled or c >= m
        ]

        def outer(k, _):
            following = pl.ds(pl.multiple_of((k + 1) * BLOCK, BLOCK), BLOCK)
            block = work[following, following] - jnp.dot(
                left[following, :], right[:, following], preferred_element_type=jnp.float32
            )
            inverse = invert_block(
                block, [functools.partial(update, k, m, c, lowest) for m, c in wanted]
            )
            prepare(k + 1, inverse, lowest)
            return 0

        lax.fori_loop(first, min(first + GROUP, blocks - 1), outer, 0)
    for k in range(blocks):
        last = k // GROUP * GROUP + GROUP
        if k + 1 < last:
            work[k * BLOCK : (k + 1) * BLOCK, (k + 1) * BLOCK : last * BLOCK] = jnp.zeros(
                (BLOCK, (last - k - 1) * BLOCK), jnp.float32
            )


VMEM = pl.BlockSpec(memory_space=pltpu.VMEM)


def factor(feat, pieces, interpret=False):
    ex_count, feat_count, rows, width = pieces.shape
    size = feat_count * width
    return pl.pallas_call(
        factor_kernel,
        in_specs=[
            pl.BlockSpec(memory_space=pltpu.SMEM),
            pl.BlockSpec(memory_space=pl.ANY),
        ],
        out_specs=[VMEM, VMEM],
        out_shape=[
            pltpu.VMEM((size, size), jnp.float32),
            pltpu.VMEM((size, BLOCK), jnp.float32),
        ],
        scratch_shapes=[
            pltpu.VMEM((ex_count, rows, size), jnp.bfloat16),
            pltpu.VMEM((CHUNK, ex_count * rows), jnp.bfloat16),
            pltpu.VMEM((4 * BLOCK, size), jnp.bfloat16),
            pltpu.VMEM((size, 4 * BLOCK), jnp.bfloat16),
            pltpu.SemaphoreType.DMA((feat_count,)),
        ],
        compiler_params=pltpu.CompilerParams(vmem_limit_bytes=36 * 2**20),
        interpret=interpret,
    )(feat, pieces)


def apply_inverse(lower, inverses, residual, column):
    size = residual.shape[1]
    blocks = size // BLOCK
    eye = lax.broadcasted_iota(jnp.int32, (BLOCK, BLOCK), 0) == lax.broadcasted_iota(
        jnp.int32, (BLOCK, BLOCK), 1
    )
    for group in range(0, blocks, GROUP):
        used = group + GROUP

        def down(k, _):
            here = pl.ds(pl.multiple_of(k * BLOCK, BLOCK), BLOCK)
            sums = jnp.zeros((BLOCK, BLOCK), jnp.float32)
            for c in range(used):
                cols = slice(c * BLOCK, (c + 1) * BLOCK)
                sums = sums + lower[here, cols] * residual[:, cols]
            middle = jnp.sum(sums, axis=1, keepdims=True)
            row = jnp.sum(inverses[here, :] * middle, axis=0, keepdims=True)
            middle = jnp.sum(jnp.where(eye, row, 0.0), axis=1, keepdims=True)
            column[here, :] = jnp.broadcast_to(middle, (BLOCK, BLOCK))
            return 0

        lax.fori_loop(group, used, down, 0, unroll=True)
    total = tuple(jnp.zeros((8, BLOCK), jnp.float32) for _ in range(blocks))
    for group in range(0, blocks, GROUP):
        used = group + GROUP

        def up(t, total):
            here = pl.ds(pl.multiple_of(t * 32, 32), 32)
            middle = column[here, :]
            fresh = list(total)
            for c in range(used):
                cols = slice(c * BLOCK, (c + 1) * BLOCK)
                product = lower[here, cols] * middle
                fresh[c] = fresh[c] + jnp.sum(product.reshape(4, 8, BLOCK), axis=0)
            return tuple(fresh)

        total = lax.fori_loop(group * BLOCK // 32, used * BLOCK // 32, up, total)
    return jnp.concatenate([jnp.sum(t, axis=0, keepdims=True) for t in total], axis=1)


def curve(rows_ref, direction):
    count, size = rows_ref.shape
    blocks = size // BLOCK
    high = 16

    def step(i, total):
        here = pl.ds(pl.multiple_of(i * high, high), high)
        tile = rows_ref[here, :].astype(jnp.float32)
        sums = jnp.zeros((high, BLOCK), jnp.float32)
        for c in range(blocks):
            cols = slice(c * BLOCK, (c + 1) * BLOCK)
            sums = sums + tile[:, cols] * direction[:, cols]
        column = jnp.sum(sums, axis=1, keepdims=True)
        fresh = list(total)
        for c in range(blocks):
            product = tile[:, c * BLOCK : (c + 1) * BLOCK] * column
            fresh[c] = fresh[c] + (product[:8] + product[8:])
        return tuple(fresh)

    total = tuple(jnp.zeros((8, BLOCK), jnp.float32) for _ in range(blocks))
    total = lax.fori_loop(0, count // high, step, total, unroll=4)
    return jnp.concatenate([jnp.sum(t, axis=0, keepdims=True) for t in total], axis=1)


def dot(left, right):
    return jnp.sum(left * right, axis=1, keepdims=True)


def first_kernel(lower, inverses, rows, residual, direction, inner, curved, column):
    solved = apply_inverse(lower, inverses, residual[...], column)
    inner[...] = dot(residual[...], solved)
    direction[...] = solved
    curved[...] = curve(rows, direction)


def next_kernel(
    total_rows, lower, inverses, rows, sums, solution, residual, direction, inner,
    solution_out, residual_out, direction_out, inner_out, curved_out, column,
):
    ahead = direction[...]
    curved = sums[...] / total_rows + (REG / D) * ahead
    size = inner[...] / dot(ahead, curved)
    solution_out[...] = solution[...] + size * ahead
    left = residual[...] - size * curved
    residual_out[...] = left
    solved = apply_inverse(lower, inverses, left, column)
    fresh = dot(left, solved)
    inner_out[...] = fresh
    direction_out[...] = solved + fresh / inner[...] * ahead
    curved_out[...] = curve(rows, direction_out)


def last_kernel(total_rows, sums, solution, direction, inner, radius, out):
    ahead = direction[...]
    curved = sums[...] / total_rows + (REG / D) * ahead
    size = inner[...] / dot(ahead, curved)
    full = solution[...] + size * ahead
    length_sq = dot(full, full)
    scale = jnp.minimum(1.0, radius[...] * math.sqrt(D) / jnp.sqrt(length_sq + 1e-06))
    out[...] = scale * full


def call(kernel, shapes, args, scratch=()):
    args = list(args)
    for place, value in enumerate(args):
        if value.size >= BLOCK * D:
            args[place] = pltpu.with_memory_space_constraint(value, pltpu.VMEM)
    return pl.pallas_call(
        kernel,
        in_specs=[VMEM] * len(args),
        out_specs=[VMEM] * len(shapes),
        out_shape=[jax.ShapeDtypeStruct(shape, jnp.float32) for shape in shapes],
        scratch_shapes=scratch,
        compiler_params=pltpu.CompilerParams(vmem_limit_bytes=8 * 2**20),
    )(*args)


def exchange(value, axis):
    count = lax.axis_size(axis)
    pieces = [value]
    for mask in range(1, count):
        pieces.append(lax.ppermute(value, axis, [(s, s ^ mask) for s in range(count)]))
    return pieces


def swap(value, axis, bit):
    mask = 2**bit
    return lax.ppermute(value, axis, [(s, s ^ mask) for s in range(lax.axis_size(axis))])


def bit_places(order):
    places = [0]
    for bit in reversed(order):
        places = places + [place | 2**bit for place in places]
    return places


def sampled_mix(samples, places, signed):
    count = lax.axis_size("ex")
    grid = samples.reshape(count * 2, -1)
    upward = list(range(1, count.bit_length() - 1))
    downward = upward[::-1]
    wanted = [(q, 0) for q in bit_places(upward)] + [(q, 1) for q in bit_places(downward)]
    numbers = jnp.array([[q ^ 1, half] for q, half in wanted] + [[q, half] for q, half in wanted])
    rows = grid[(numbers[:, 0] ^ lax.axis_index("ex")) * 2 + numbers[:, 1]].reshape(2, -1)

    def mix(chosen):
        odd = lax.population_count(chosen[:, None] & places[None, :]) & 1
        table = (1 - 2 * odd).astype(jnp.bfloat16)
        return jnp.dot(table, signed, preferred_element_type=jnp.float32)

    total = swap(mix(rows[0]).astype(jnp.float16), "ex", 0).astype(jnp.float32) + mix(rows[1])
    parts = list(jnp.split(total, 2))
    for bits in zip(upward, downward):
        halves = [jnp.split(part, 2) for part in parts]
        got = [
            swap(half[1].astype(jnp.float16), "ex", bit) for half, bit in zip(halves, bits)
        ]
        got = lax.optimization_barrier(got)
        parts = [half[0] + other.astype(jnp.float32) for half, other in zip(halves, got)]
    return parts


def butterfly(value, axes=("ex", "feat")):
    for axis in axes:
        count = lax.axis_size(axis)
        for bit in range(count.bit_length() - 1):
            value = value + swap(value, axis, bit)
    return value


def local(features, weights, labels, signs, samples, radius):
    highest = lax.Precision.HIGHEST
    row_count, feat_width = features.shape
    ex_count = lax.axis_size("ex")
    ex_index = lax.axis_index("ex")
    feat_count = lax.axis_size("feat")
    feat_index = lax.axis_index("feat")
    total_rows = row_count * ex_count
    sample_count = samples.shape[0]
    dense = features.astype(jnp.float32)
    margins = butterfly(jnp.dot(dense, weights, precision=highest), ("feat",))
    probability = 1.0 / (1.0 + jnp.exp(-margins))
    curvature = probability * (1.0 - probability)
    weighted = (jnp.sqrt(curvature)[:, None] * dense).astype(jnp.bfloat16)
    signed = weighted * signs.astype(jnp.bfloat16)[:, None]
    places = ex_index * row_count + lax.iota(jnp.int32, row_count)
    scale = 1.0 / math.sqrt(total_rows * sample_count)
    sketch = (jnp.concatenate(sampled_mix(samples, places, signed)) * scale).astype(jnp.bfloat16)
    wide_sketch = jnp.stack(exchange(sketch, "feat"))
    pieces = lax.all_gather(wide_sketch, "ex", axis=0)
    lower, inverses = factor(feat_index.astype(jnp.int32)[None], pieces)

    grad_part = jnp.dot(probability - labels.astype(jnp.float32), dense, precision=highest)
    own_weights = jnp.where(ex_index == 0, REG / D, 0.0) * weights
    wide = jnp.zeros((feat_count, feat_width), jnp.float32)
    wide = lax.dynamic_update_slice_in_dim(
        wide, (grad_part / total_rows + own_weights)[None], feat_index, 0
    )
    residual = -butterfly(wide.reshape(1, D))
    own_rows = lax.all_to_all(weighted, "feat", split_axis=0, concat_axis=1, tiled=True)

    row, one = (1, D), (1, 1)
    scratch = [pltpu.VMEM((D, BLOCK), jnp.float32)]
    direction, inner, curved = call(
        first_kernel, [row, one, row], [lower, inverses, own_rows, residual], scratch
    )
    solution = jnp.zeros(row, jnp.float32)
    following = functools.partial(next_kernel, total_rows)
    for _ in range(ITERS - 1):
        solution, residual, direction, inner, curved = call(
            following,
            [row, row, row, one, row],
            [lower, inverses, own_rows, butterfly(curved), solution, residual, direction, inner],
            scratch,
        )
    (step,) = call(
        functools.partial(last_kernel, total_rows),
        [row],
        [butterfly(curved), solution, direction, inner, radius[None, :]],
    )
    own = lax.dynamic_slice_in_dim(step[0], feat_index * feat_width, feat_width, 0)
    return weights + own


def solution(mesh):
    in_specs = (P("ex", "feat"), P("feat"), P("ex"), P("ex"), P(), P())
    out_specs = P("feat")
    return jax.shard_map(local, mesh=mesh, in_specs=in_specs, out_specs=out_specs, check_vma=False)
```

```python
import functools
import math

import jax
import jax.numpy as jnp
from jax import lax
from jax.experimental import pallas as pl
from jax.experimental.pallas import tpu as pltpu
from jax.sharding import PartitionSpec as P

D = 2048
ITERS = 4
REG = 0.02
BLOCK = 128
PIVOTS = 8
CHUNK = 256
GROUP = 4


def split(value):
    high = value.astype(jnp.bfloat16)
    low = (value - high.astype(jnp.float32)).astype(jnp.bfloat16)
    return high, low


def invert_block(block, pieces=()):
    tiles = BLOCK // PIVOTS
    slots = BLOCK // 2
    lane = lax.broadcasted_iota(jnp.int32, (PIVOTS, BLOCK), 1)
    sub = lax.broadcasted_iota(jnp.int32, (PIVOTS, BLOCK), 0)
    shape = (PIVOTS, BLOCK)
    held = [block[t * PIVOTS : (t + 1) * PIVOTS, :] for t in range(tiles)]
    plain, scaled_rows = [], []
    for step in range(tiles):
        first = step * PIVOTS
        rows = held[step]
        inside = (lane >= first) & (lane < first + PIVOTS)
        before = lane < first + PIVOTS
        last = step + 1 == tiles

        def columns(tile):
            return [
                jnp.broadcast_to(tile[:, first + j : first + j + 1], shape) for j in range(PIVOTS)
            ]

        wide = columns(rows)
        cell = {}
        for j in range(PIVOTS):
            for i in range(j, PIVOTS):
                cell[i, j] = jnp.broadcast_to(wide[j][i : i + 1, :], shape)
        rows = jnp.where(inside, (lane - first == sub).astype(jnp.float32), rows)
        line = [jnp.broadcast_to(rows[i : i + 1, :], shape) for i in range(PIVOTS)]
        if not last:
            ahead = columns(held[step + 1])
            total = jnp.where(inside, 0.0, held[step + 1])
        scaled = {}
        pairs = []
        for j in range(0, PIVOTS, 2):
            a, b, d = cell[j, j], cell[j + 1, j], cell[j + 1, j + 1]
            inverse = 1.0 / (a * d - b * b)
            slot = (step * PIVOTS + j) // 2
            for piece in pieces[slot * len(pieces) // slots : (slot + 1) * len(pieces) // slots]:
                piece()
            pairs.append((a * inverse, b * inverse, d * inverse))
            for i in range(j + 2, PIVOTS):
                one, two = cell[i, j], cell[i, j + 1]
                scaled[i, j] = one * d - two * b
                scaled[i, j + 1] = two * a - one * b
            for i in range(j + 2, PIVOTS):
                for m in range(j + 2, i + 1):
                    product = scaled[i, j] * cell[m, j] + scaled[i, j + 1] * cell[m, j + 1]
                    cell[i, m] = cell[i, m] - product * inverse
            if not last:
                one = ahead[j] * d - ahead[j + 1] * b
                two = ahead[j + 1] * a - ahead[j] * b
                for m in range(j + 2, PIVOTS):
                    product = one * cell[m, j] + two * cell[m, j + 1]
                    ahead[m] = ahead[m] - product * inverse
                total = total - (one * line[j] + two * line[j + 1]) * inverse
            for i in range(j + 2, PIVOTS):
                scaled[i, j] = scaled[i, j] * inverse
                scaled[i, j + 1] = scaled[i, j + 1] * inverse
                line[i] = line[i] - (scaled[i, j] * line[j] + scaled[i, j + 1] * line[j + 1])
        if not last:
            held[step + 1] = total
        for j in range(PIVOTS - 2, -1, -2):
            a, b, d = pairs[j // 2]
            one = line[j] * d - line[j + 1] * b
            two = line[j + 1] * a - line[j] * b
            for i in range(j + 2, PIVOTS):
                one = one - scaled[i, j] * line[i]
                two = two - scaled[i, j + 1] * line[i]
            line[j], line[j + 1] = one, two
        for t in range(step + 2, tiles):
            total = jnp.where(inside, 0.0, held[t])
            for j, column in enumerate(columns(held[t])):
                total = total - column * line[j]
            held[t] = total
        plain.append(jnp.where(before, rows, 0.0))
        rows = line[0]
        for j in range(1, PIVOTS):
            rows = jnp.where(sub == j, line[j], rows)
        scaled_rows.append(jnp.where(before, rows, 0.0))
    high, low = split(jnp.concatenate(plain, axis=0))
    left = jnp.concatenate([high, low, high, low], axis=0)
    high, low = split(jnp.concatenate(scaled_rows, axis=0))
    right = jnp.concatenate([high, high, low, low], axis=0)
    return lax.dot_general(
        left, right, (((0,), (0,)), ((), ())), preferred_element_type=jnp.float32
    )


def factor_kernel(feat, pieces, work, inv_ref, sketch, turned, right, left, sem):
    size = work.shape[0]
    blocks = size // BLOCK
    feat_count = pieces.shape[1]
    width = size // feat_count
    copies = []
    for mask in range(feat_count):
        start = pl.multiple_of((feat[0] ^ mask) * width, width)
        copies.append(
            pltpu.make_async_copy(
                pieces.at[:, mask], sketch.at[:, :, pl.ds(start, width)], sem.at[mask]
            )
        )
    for copy in copies:
        copy.start()
    for copy in copies:
        copy.wait()
    samples = sketch.shape[0] * sketch.shape[1]
    chunks = size // CHUNK

    def chunk(c):
        return slice(c * CHUNK, (c + 1) * CHUNK)

    def gram(m, _):
        start = pl.multiple_of(m * CHUNK, CHUNK)
        here = pl.ds(start, CHUNK)
        turned[...] = sketch[:, :, here].reshape(samples, CHUNK).T
        for c in range(chunks):

            @pl.when(c >= m)
            def _():
                product = jnp.dot(
                    turned[...],
                    sketch[:, :, chunk(c)].reshape(samples, CHUNK),
                    preferred_element_type=jnp.float32,
                )
                row = start + lax.broadcasted_iota(jnp.int32, product.shape, 0)
                col = c * CHUNK + lax.broadcasted_iota(jnp.int32, product.shape, 1)
                work[here, chunk(c)] = jnp.where(row == col, product + REG / D, product)

        return 0

    lax.fori_loop(0, chunks, gram, 0)

    eye = (
        lax.broadcasted_iota(jnp.int32, (BLOCK, BLOCK), 0)
        == lax.broadcasted_iota(jnp.int32, (BLOCK, BLOCK), 1)
    ).astype(jnp.float32)

    def prepare(k, inverse, lowest):
        here = pl.ds(pl.multiple_of(k * BLOCK, BLOCK), BLOCK)
        inv_ref[here, :] = inverse
        high, low = split(inverse)
        diag = jnp.concatenate([high, high, low, low], axis=0)
        work[here, here] = eye
        for c in range(chunks):
            panel = work[here, chunk(c)]
            high, low = split(panel)
            right[0:BLOCK, chunk(c)] = high
            right[BLOCK : 2 * BLOCK, chunk(c)] = high
            right[2 * BLOCK : 3 * BLOCK, chunk(c)] = low
            right[3 * BLOCK : 4 * BLOCK, chunk(c)] = low
            if c >= lowest:
                high, low = split(panel.T)
                wide = jnp.concatenate([high, low, high, low], axis=1)
                scaled = jnp.dot(wide, diag, preferred_element_type=jnp.float32)
                place = c * CHUNK + lax.broadcasted_iota(jnp.int32, (CHUNK, BLOCK), 0)
                high, low = split(jnp.where(place >= (k + 1) * BLOCK, scaled, 0.0))
                left[chunk(c), :] = jnp.concatenate([high, low, high, low], axis=1)

    def update(k, m, c, lowest):
        product = jnp.dot(
            left[chunk(m), :], right[:, chunk(c)], preferred_element_type=jnp.float32
        )
        value = work[chunk(m), chunk(c)]
        if lowest <= c < lowest + GROUP * BLOCK // CHUNK:
            row = m * CHUNK + lax.broadcasted_iota(jnp.int32, value.shape, 0)
            col = c * CHUNK + lax.broadcasted_iota(jnp.int32, value.shape, 1)
            fresh = (col >= k * BLOCK) & (col < (k + 1) * BLOCK) & (row >= (k + 1) * BLOCK)
            value = jnp.where(fresh, 0.0, value)
        work[chunk(m), chunk(c)] = value - product

    prepare(0, invert_block(work[0:BLOCK, 0:BLOCK]), 0)
    for first in range(0, blocks, GROUP):
        lowest = first * BLOCK // CHUNK
        settled = lowest + GROUP * BLOCK // CHUNK
        wanted = [
            (m, c) for m in range(lowest, chunks) for c in range(chunks) if c < settled or c >= m
        ]

        def outer(k, _):
            following = pl.ds(pl.multiple_of((k + 1) * BLOCK, BLOCK), BLOCK)
            block = work[following, following] - jnp.dot(
                left[following, :], right[:, following], preferred_element_type=jnp.float32
            )
            inverse = invert_block(
                block, [functools.partial(update, k, m, c, lowest) for m, c in wanted]
            )
            prepare(k + 1, inverse, lowest)
            return 0

        lax.fori_loop(first, min(first + GROUP, blocks - 1), outer, 0)
    for k in range(blocks):
        last = k // GROUP * GROUP + GROUP
        if k + 1 < last:
            work[k * BLOCK : (k + 1) * BLOCK, (k + 1) * BLOCK : last * BLOCK] = jnp.zeros(
                (BLOCK, (last - k - 1) * BLOCK), jnp.float32
            )


VMEM = pl.BlockSpec(memory_space=pltpu.VMEM)


def factor(feat, pieces, interpret=False):
    ex_count, feat_count, rows, width = pieces.shape
    size = feat_count * width
    return pl.pallas_call(
        factor_kernel,
        in_specs=[
            pl.BlockSpec(memory_space=pltpu.SMEM),
            pl.BlockSpec(memory_space=pl.ANY),
        ],
        out_specs=[VMEM, VMEM],
        out_shape=[
            pltpu.VMEM((size, size), jnp.float32),
            pltpu.VMEM((size, BLOCK), jnp.float32),
        ],
        scratch_shapes=[
            pltpu.VMEM((ex_count, rows, size), jnp.bfloat16),
            pltpu.VMEM((CHUNK, ex_count * rows), jnp.bfloat16),
            pltpu.VMEM((4 * BLOCK, size), jnp.bfloat16),
            pltpu.VMEM((size, 4 * BLOCK), jnp.bfloat16),
            pltpu.SemaphoreType.DMA((feat_count,)),
        ],
        compiler_params=pltpu.CompilerParams(vmem_limit_bytes=36 * 2**20),
        interpret=interpret,
    )(feat, pieces)


def apply_inverse(lower, inverses, residual, column):
    size = residual.shape[1]
    blocks = size // BLOCK
    eye = lax.broadcasted_iota(jnp.int32, (BLOCK, BLOCK), 0) == lax.broadcasted_iota(
        jnp.int32, (BLOCK, BLOCK), 1
    )
    for group in range(0, blocks, GROUP):
        used = group + GROUP

        def down(k, _):
            here = pl.ds(pl.multiple_of(k * BLOCK, BLOCK), BLOCK)
            sums = jnp.zeros((BLOCK, BLOCK), jnp.float32)
            for c in range(used):
                cols = slice(c * BLOCK, (c + 1) * BLOCK)
                sums = sums + lower[here, cols] * residual[:, cols]
            middle = jnp.sum(sums, axis=1, keepdims=True)
            row = jnp.sum(inverses[here, :] * middle, axis=0, keepdims=True)
            middle = jnp.sum(jnp.where(eye, row, 0.0), axis=1, keepdims=True)
            column[here, :] = jnp.broadcast_to(middle, (BLOCK, BLOCK))
            return 0

        lax.fori_loop(group, used, down, 0, unroll=True)
    total = tuple(jnp.zeros((8, BLOCK), jnp.float32) for _ in range(blocks))
    for group in range(0, blocks, GROUP):
        used = group + GROUP

        def up(t, total):
            here = pl.ds(pl.multiple_of(t * 32, 32), 32)
            middle = column[here, :]
            fresh = list(total)
            for c in range(used):
                cols = slice(c * BLOCK, (c + 1) * BLOCK)
                product = lower[here, cols] * middle
                fresh[c] = fresh[c] + jnp.sum(product.reshape(4, 8, BLOCK), axis=0)
            return tuple(fresh)

        total = lax.fori_loop(group * BLOCK // 32, used * BLOCK // 32, up, total)
    return jnp.concatenate([jnp.sum(t, axis=0, keepdims=True) for t in total], axis=1)


def curve(rows_ref, direction):
    parts, count, width = rows_ref.shape
    size = parts * width
    blocks = size // BLOCK
    high = 16

    def step(i, total):
        here = pl.ds(pl.multiple_of(i * high, high), high)
        tile = jnp.concatenate([rows_ref[q, here, :] for q in range(parts)], axis=1)
        tile = tile.astype(jnp.float32)
        sums = jnp.zeros((high, BLOCK), jnp.float32)
        for c in range(blocks):
            cols = slice(c * BLOCK, (c + 1) * BLOCK)
            sums = sums + tile[:, cols] * direction[:, cols]
        column = jnp.sum(sums, axis=1, keepdims=True)
        fresh = list(total)
        for c in range(blocks):
            product = tile[:, c * BLOCK : (c + 1) * BLOCK] * column
            fresh[c] = fresh[c] + (product[:8] + product[8:])
        return tuple(fresh)

    total = tuple(jnp.zeros((8, BLOCK), jnp.float32) for _ in range(blocks))
    total = lax.fori_loop(0, count // high, step, total, unroll=4)
    return jnp.concatenate([jnp.sum(t, axis=0, keepdims=True) for t in total], axis=1)


def dot(left, right):
    return jnp.sum(left * right, axis=1, keepdims=True)


def first_kernel(lower, inverses, rows, residual, direction, inner, curved, column):
    solved = apply_inverse(lower, inverses, residual[...], column)
    inner[...] = dot(residual[...], solved)
    direction[...] = solved
    curved[...] = curve(rows, direction)


def next_kernel(
    total_rows, lower, inverses, rows, sums, solution, residual, direction, inner,
    solution_out, residual_out, direction_out, inner_out, curved_out, column,
):
    ahead = direction[...]
    curved = sums[...] / total_rows + (REG / D) * ahead
    size = inner[...] / dot(ahead, curved)
    solution_out[...] = solution[...] + size * ahead
    left = residual[...] - size * curved
    residual_out[...] = left
    solved = apply_inverse(lower, inverses, left, column)
    fresh = dot(left, solved)
    inner_out[...] = fresh
    direction_out[...] = solved + fresh / inner[...] * ahead
    curved_out[...] = curve(rows, direction_out)


def last_kernel(total_rows, sums, solution, direction, inner, radius, out):
    ahead = direction[...]
    curved = sums[...] / total_rows + (REG / D) * ahead
    size = inner[...] / dot(ahead, curved)
    full = solution[...] + size * ahead
    length_sq = dot(full, full)
    scale = jnp.minimum(1.0, radius[...] * math.sqrt(D) / jnp.sqrt(length_sq + 1e-06))
    out[...] = scale * full


def call(kernel, shapes, args, scratch=()):
    args = list(args)
    for place, value in enumerate(args):
        if value.size >= BLOCK * D:
            args[place] = pltpu.with_memory_space_constraint(value, pltpu.VMEM)
    return pl.pallas_call(
        kernel,
        in_specs=[VMEM] * len(args),
        out_specs=[VMEM] * len(shapes),
        out_shape=[jax.ShapeDtypeStruct(shape, jnp.float32) for shape in shapes],
        scratch_shapes=scratch,
        compiler_params=pltpu.CompilerParams(vmem_limit_bytes=8 * 2**20),
    )(*args)


def exchange(value, axis):
    count = lax.axis_size(axis)
    pieces = [value]
    for mask in range(1, count):
        pieces.append(lax.ppermute(value, axis, [(s, s ^ mask) for s in range(count)]))
    return pieces


def swap(value, axis, bit):
    mask = 2**bit
    return lax.ppermute(value, axis, [(s, s ^ mask) for s in range(lax.axis_size(axis))])


def bit_places(order):
    places = [0]
    for bit in reversed(order):
        places = places + [place | 2**bit for place in places]
    return places


def sampled_mix(samples, places, signed):
    count = lax.axis_size("ex")
    grid = samples.reshape(count * 2, -1)
    upward = list(range(1, count.bit_length() - 1))
    downward = upward[::-1]
    wanted = [(q, 0) for q in bit_places(upward)] + [(q, 1) for q in bit_places(downward)]
    numbers = jnp.array([[q ^ 1, half] for q, half in wanted] + [[q, half] for q, half in wanted])
    rows = grid[(numbers[:, 0] ^ lax.axis_index("ex")) * 2 + numbers[:, 1]].reshape(2, -1)

    def mix(chosen):
        odd = lax.population_count(chosen[:, None] & places[None, :]) & 1
        table = (1 - 2 * odd).astype(jnp.bfloat16)
        return jnp.dot(table, signed, preferred_element_type=jnp.float32)

    total = swap(mix(rows[0]).astype(jnp.float16), "ex", 0).astype(jnp.float32) + mix(rows[1])
    parts = list(jnp.split(total, 2))
    for bits in zip(upward, downward):
        halves = [jnp.split(part, 2) for part in parts]
        got = [
            swap(half[1].astype(jnp.float16), "ex", bit) for half, bit in zip(halves, bits)
        ]
        got = lax.optimization_barrier(got)
        parts = [half[0] + other.astype(jnp.float32) for half, other in zip(halves, got)]
    return parts


def butterfly(value, axes=("ex", "feat")):
    for axis in axes:
        count = lax.axis_size(axis)
        for bit in range(count.bit_length() - 1):
            value = value + swap(value, axis, bit)
    return value


def local(features, weights, labels, signs, samples, radius):
    highest = lax.Precision.HIGHEST
    row_count, feat_width = features.shape
    ex_count = lax.axis_size("ex")
    ex_index = lax.axis_index("ex")
    feat_count = lax.axis_size("feat")
    feat_index = lax.axis_index("feat")
    total_rows = row_count * ex_count
    sample_count = samples.shape[0]
    dense = features.astype(jnp.float32)
    margins = butterfly(jnp.dot(dense, weights, precision=highest), ("feat",))
    probability = 1.0 / (1.0 + jnp.exp(-margins))
    curvature = probability * (1.0 - probability)
    weighted = (jnp.sqrt(curvature)[:, None] * dense).astype(jnp.bfloat16)
    signed = weighted * signs.astype(jnp.bfloat16)[:, None]
    places = ex_index * row_count + lax.iota(jnp.int32, row_count)
    scale = 1.0 / math.sqrt(total_rows * sample_count)
    sketch = (jnp.concatenate(sampled_mix(samples, places, signed)) * scale).astype(jnp.bfloat16)
    wide_sketch = jnp.stack(exchange(sketch, "feat"))
    pieces = lax.all_gather(wide_sketch, "ex", axis=0)
    lower, inverses = factor(feat_index.astype(jnp.int32)[None], pieces)

    grad_part = jnp.dot(probability - labels.astype(jnp.float32), dense, precision=highest)
    own_weights = jnp.where(ex_index == 0, REG / D, 0.0) * weights
    wide = jnp.zeros((feat_count, feat_width), jnp.float32)
    wide = lax.dynamic_update_slice_in_dim(
        wide, (grad_part / total_rows + own_weights)[None], feat_index, 0
    )
    residual = -butterfly(wide.reshape(1, D))
    own_rows = lax.all_to_all(
        weighted.reshape(feat_count, -1, feat_width), "feat", split_axis=0, concat_axis=0, tiled=True
    )

    row, one = (1, D), (1, 1)
    scratch = [pltpu.VMEM((D, BLOCK), jnp.float32)]
    direction, inner, curved = call(
        first_kernel, [row, one, row], [lower, inverses, own_rows, residual], scratch
    )
    solution = jnp.zeros(row, jnp.float32)
    following = functools.partial(next_kernel, total_rows)
    for _ in range(ITERS - 1):
        solution, residual, direction, inner, curved = call(
            following,
            [row, row, row, one, row],
            [lower, inverses, own_rows, butterfly(curved), solution, residual, direction, inner],
            scratch,
        )
    (step,) = call(
        functools.partial(last_kernel, total_rows),
        [row],
        [butterfly(curved), solution, direction, inner, radius[None, :]],
    )
    own = lax.dynamic_slice_in_dim(step[0], feat_index * feat_width, feat_width, 0)
    return weights + own


def solution(mesh):
    in_specs = (P("ex", "feat"), P("feat"), P("ex"), P("ex"), P(), P())
    out_specs = P("feat")
    return jax.shard_map(local, mesh=mesh, in_specs=in_specs, out_specs=out_specs, check_vma=False)
```
